32 devices in a mesh: row: 4 (over y, core), col: 8 (over z, x).
Axes of the slice: x: 2, y: 2, z: 4, core: 2. Of those that a mesh axis runs over, the one named last changes fastest.
Arguments:
- embedding: bfloat16 [512, 128], P('row'), may hold values from -6 to 6
- kernel: bfloat16 [3, 3, 64, 64], replicated, may hold values from -0.25 to 0.25
- cotangent: bfloat16 [512, 512, 64], P('row', 'col'), may hold values from -6 to 6
Outputs:
- prediction: float32 [512, 512, 64], P('row', 'col')
- grad_kernel: float32 [3, 3, 64, 64], replicated
- grad_embedding: float32 [512, 128], P('row')
The draws below stay inside these ranges and needn't reach their ends.
All inputs are finite; a program needn't handle non-finite values.
Results may differ from the reference program's by a relative error of at most 0.0031.
Values may be sent and summed in bfloat16 or wider, within the bound.
A program may use at most 128 MiB of HBM per device.

```python
import jax
import jax.numpy as jnp
from jax import lax

PAIR_CHANNELS = 64
DILATION_STEP = 8
REGION_BINS = 512
DEVICE_ROW_BINS = 128
N_ROW = 4


def shard_levels(key, shape, pieces, smallest, largest):
    gain, own = 1.0, jax.random.fold_in(key, 6)
    for dim, parts in pieces:
        steps = jnp.exp(jax.random.uniform(jax.random.fold_in(own, dim), (parts,), jnp.float32, smallest / len(pieces), largest / len(pieces)))
        gain = gain * jnp.repeat(steps, shape[dim] // parts).reshape([-1 if axis == dim else 1 for axis in range(len(shape))])
    return gain


def bell_draw(own_key, extent, deviation, bound, split=(), kind=jnp.bfloat16):
    level = shard_levels(own_key, extent, split, -0.22, 0.18) if split else 1.0
    drawn = jax.random.normal(own_key, extent, jnp.float32) * deviation * level
    return jnp.minimum(jnp.maximum(drawn, -bound), bound).astype(kind)


def setup_inputs(seed: int = 0) -> dict:
    seeds = jax.random.split(jax.random.key(seed), 4)
    embedding = bell_draw(seeds[0], (REGION_BINS, 2 * PAIR_CHANNELS), 1.0, 6.0, ((0, 4),))
    kernel = bell_draw(seeds[1], (3, 3, PAIR_CHANNELS, PAIR_CHANNELS), (9 * PAIR_CHANNELS) ** -0.5, 0.25)
    cotangent = bell_draw(seeds[2], (REGION_BINS, REGION_BINS, PAIR_CHANNELS), 1.0, 6.0, ((0, 4), (1, 8)))
    return {"embedding": embedding, "kernel": kernel, "cotangent": cotangent}


def reference(embedding, kernel, cotangent):
    whole_region = embedding.astype(jnp.float32)
    embedding_padded = jnp.pad(whole_region, ((DILATION_STEP, DILATION_STEP), (0, 0)))
    inside_mask = jnp.pad(jnp.ones((REGION_BINS,), jnp.float32), (DILATION_STEP, DILATION_STEP))
    col_mult = embedding_padded[:, :PAIR_CHANNELS]
    col_add = embedding_padded[:, PAIR_CHANNELS:]
    cotangent_padded = jnp.pad(cotangent, ((DILATION_STEP, DILATION_STEP), (DILATION_STEP, DILATION_STEP), (0, 0)))
    weights = kernel.astype(jnp.float32)

    def block(totals, block_index):
        kernel_acc, col_acc = totals
        row_offset = block_index.astype(jnp.int32) * DEVICE_ROW_BINS
        row_embedding = lax.dynamic_slice_in_dim(embedding_padded, row_offset, DEVICE_ROW_BINS + 2 * DILATION_STEP, 0)
        row_inside_mask = lax.dynamic_slice_in_dim(inside_mask, row_offset, DEVICE_ROW_BINS + 2 * DILATION_STEP, 0)
        preactivation_wide = row_embedding[:, None, :PAIR_CHANNELS] * col_mult[None] + row_embedding[:, None, PAIR_CHANNELS:] + col_add[None]
        mask = row_inside_mask[:, None, None] * inside_mask[None, :, None]
        activation_wide = (jax.nn.silu(preactivation_wide) * mask).astype(jnp.bfloat16).astype(jnp.float32)
        cotangent_wide = lax.dynamic_slice_in_dim(cotangent_padded, row_offset, DEVICE_ROW_BINS + 2 * DILATION_STEP, 0).astype(jnp.float32)
        cotangent_local = cotangent_wide[DILATION_STEP:DILATION_STEP + DEVICE_ROW_BINS, DILATION_STEP:DILATION_STEP + REGION_BINS]
        forward = jnp.zeros((DEVICE_ROW_BINS, REGION_BINS, PAIR_CHANNELS), jnp.float32)
        backward = jnp.zeros((DEVICE_ROW_BINS, REGION_BINS, PAIR_CHANNELS), jnp.float32)
        kernel_rows = []
        for kernel_tap_row in range(3):
            kernel_cols = []
            for kernel_tap_column in range(3):
                shifted_pairs = activation_wide[kernel_tap_row * DILATION_STEP:kernel_tap_row * DILATION_STEP + DEVICE_ROW_BINS, kernel_tap_column * DILATION_STEP:kernel_tap_column * DILATION_STEP + REGION_BINS]
                forward = forward + jnp.einsum('ijc,cd->ijd', shifted_pairs, weights[kernel_tap_row, kernel_tap_column])
                kernel_cols.append(jnp.einsum('ijc,ijd->cd', shifted_pairs, cotangent_local))
                cotangent_shifted = cotangent_wide[(2 - kernel_tap_row) * DILATION_STEP:(2 - kernel_tap_row) * DILATION_STEP + DEVICE_ROW_BINS, (2 - kernel_tap_column) * DILATION_STEP:(2 - kernel_tap_column) * DILATION_STEP + REGION_BINS]
                backward = backward + jnp.einsum('ijd,cd->ijc', cotangent_shifted, weights[kernel_tap_row, kernel_tap_column])
            kernel_rows.append(jnp.stack(kernel_cols))
        kernel_acc = kernel_acc + jnp.stack(kernel_rows)
        preactivation = preactivation_wide[DILATION_STEP:DILATION_STEP + DEVICE_ROW_BINS, DILATION_STEP:DILATION_STEP + REGION_BINS]
        sigmoid_val = jax.nn.sigmoid(preactivation)
        grad_pre = backward * sigmoid_val * (1.0 + preactivation * (1.0 - sigmoid_val))
        row_multiplier = row_embedding[DILATION_STEP:DILATION_STEP + DEVICE_ROW_BINS, :PAIR_CHANNELS]
        col_real = whole_region[:, :PAIR_CHANNELS]
        row_part = jnp.concatenate([jnp.sum(grad_pre * col_real[None], axis=1), jnp.sum(grad_pre, axis=1)], axis=1)
        col_part = jnp.concatenate([jnp.sum(grad_pre * row_multiplier[:, None], axis=0), jnp.sum(grad_pre, axis=0)], axis=1)
        return (kernel_acc, col_acc + col_part), (forward, row_part)

    start_totals = (jnp.zeros((3, 3, PAIR_CHANNELS, PAIR_CHANNELS), jnp.float32), jnp.zeros((REGION_BINS, 2 * PAIR_CHANNELS), jnp.float32))
    totals, stacked = lax.scan(block, start_totals, jnp.arange(N_ROW))
    kernel_acc, col_acc = totals
    forwards, row_parts = stacked
    prediction = forwards.reshape(REGION_BINS, REGION_BINS, PAIR_CHANNELS)
    grad_kernel = kernel_acc / REGION_BINS
    grad_embedding = (row_parts.reshape(REGION_BINS, 2 * PAIR_CHANNELS) + col_acc) * (REGION_BINS ** -0.5)
    return prediction, grad_kernel, grad_embedding
```

```python
import functools

import jax
import jax.numpy as jnp
from jax import lax
from jax.experimental import pallas as pl
from jax.experimental.pallas import tpu as pltpu
from jax.sharding import PartitionSpec as P

STEP = 8
MESH = pl.DeviceIdType.MESH
VMEM = pl.BlockSpec(memory_space=pltpu.VMEM)
ANY = pl.BlockSpec(memory_space=pl.ANY)


def signal(barrier, row, col):
    pl.semaphore_signal(barrier, inc=1, device_id=(row, col), device_id_type=MESH)


def remote(src, dst, send, recv, row, col):
    return pltpu.make_async_remote_copy(
        src_ref=src,
        dst_ref=dst,
        send_sem=send,
        recv_sem=recv,
        device_id=(row, col),
        device_id_type=MESH,
    )


def gather_kernel(n_row, emb_ref, out_ref, held, send_sem, recv_sem):
    row, col = lax.axis_index("row"), lax.axis_index("col")
    rows = emb_ref.shape[0]
    barrier = pltpu.get_barrier_semaphore()
    peers = [lax.rem(row + d, n_row) for d in range(1, n_row)]
    for peer in peers:
        signal(barrier, peer, col)
    pl.semaphore_wait(barrier, n_row - 1)
    copies = []
    for d, peer in enumerate(peers):
        copy = remote(emb_ref, held.at[d], send_sem.at[d], recv_sem.at[d], peer, col)
        copy.start()
        copies.append(copy)
    border = jnp.zeros((STEP, out_ref.shape[1]), jnp.float32)
    out_ref[:STEP] = border
    out_ref[STEP + n_row * rows :] = border
    out_ref[pl.ds(pl.multiple_of(STEP + row * rows, STEP), rows)] = emb_ref[...].astype(jnp.float32)
    for d, copy in enumerate(copies):
        copy.wait()
        owner = lax.rem(row + n_row - 1 - d, n_row)
        out_ref[pl.ds(pl.multiple_of(STEP + owner * rows, STEP), rows)] = held[d].astype(
            jnp.float32
        )


def tile_kernel(
    n_row,
    chunk,
    wide_ref,
    kernel_ref,
    cot_hbm,
    pred_hbm,
    part_ref,
    cot_ref,
    pred_ref,
    weight_ref,
    u_row_ref,
    v_row_ref,
    act_ref,
    slope_ref,
    grad_ref,
    product_ref,
    u_sum_ref,
    v_sum_ref,
    bins_ref,
    flat_ref,
    packed_ref,
    cot_sem,
    pred_sem,
):
    rows, columns, channels = cot_ref.shape
    half = rows // 2
    blocks = half // STEP
    span = columns + 2 * STEP
    lanes = 2 * channels
    bins = n_row * rows
    row0 = lax.axis_index("row") * rows
    col0 = lax.axis_index("col") * columns

    def cot_copy(n, h):
        at = pl.ds(h * half + n * STEP, STEP)
        return pltpu.make_async_copy(cot_hbm.at[at], cot_ref.at[at], cot_sem.at[n, h])

    def pred_copy(n, h):
        at = pl.ds(h * half + n * STEP, STEP)
        return pltpu.make_async_copy(pred_ref.at[at], pred_hbm.at[at], pred_sem.at[n, h])

    for n in range(blocks):
        for h in range(2):
            cot_copy(n, h).start()

    none = jnp.zeros((channels, channels), jnp.float32)
    for a in range(3):
        for b in range(3):
            w = kernel_ref[a, b].astype(jnp.float32)
            both = jnp.concatenate(
                [jnp.concatenate([w, none], axis=1), jnp.concatenate([none, w], axis=1)], axis=0
            )
            weight_ref[a * lanes : (a + 1) * lanes, b * lanes : (b + 1) * lanes] = both.astype(
                jnp.bfloat16
            )

    def first(shape):
        return lax.broadcasted_iota(jnp.int32, shape, len(shape) - 1) < channels

    def swap(x):
        return pltpu.roll(x, channels, 1)

    depth = half + 2 * STEP
    low = wide_ref[pl.ds(pl.multiple_of(row0, STEP), depth)]
    high = wide_ref[pl.ds(pl.multiple_of(row0 + half, STEP), depth)]
    in_first = first((depth, lanes))
    u_row_ref[...] = jnp.where(in_first, low, swap(high))
    v_row_ref[...] = jnp.where(in_first, swap(low), high)
    cols = wide_ref[pl.ds(pl.multiple_of(col0, STEP), span)]
    in_first_col = first((span, lanes))
    u_col = jnp.where(in_first_col, cols, swap(cols))
    v_col = jnp.where(in_first_col, swap(cols), cols)
    col_pos = col0 - STEP + lax.broadcasted_iota(jnp.int32, (span, lanes), 0)
    col_in = jnp.where((col_pos >= 0) & (col_pos < bins), 1.0, 0.0)

    def activate(m, carry):
        at = pl.ds(pl.multiple_of(m * STEP, STEP), STEP)
        shape = (STEP, 1, lanes)
        pos = row0 - STEP + m * STEP + lax.broadcasted_iota(jnp.int32, shape, 0)
        pos = pos + jnp.where(first(shape), 0, half)
        row_in = jnp.where((pos >= 0) & (pos < bins), 1.0, 0.0)
        pairs = u_row_ref[at][:, None, :] * u_col[None] + v_row_ref[at][:, None, :] + v_col[None]
        s = 0.5 * jnp.tanh(0.5 * pairs) + 0.5
        s = s * (row_in * col_in[None])
        act = pairs * s
        act_ref[m] = act.reshape(STEP * span, lanes).astype(jnp.bfloat16)
        slope_ref[m] = s + act * (1.0 - s)
        grad_ref[m] = jnp.zeros((STEP, span, lanes), jnp.float32)
        return carry

    lax.fori_loop(0, blocks + 2, activate, 0)
    product_ref[...] = jnp.zeros_like(product_ref)

    def convolve(n, carry):
        for h in range(2):
            cot_copy(n, h).wait()
        at = [pl.ds(pl.multiple_of(h * half + n * STEP, STEP), STEP) for h in range(2)]
        x = jnp.concatenate([act_ref[n + a] for a in range(3)], axis=1)
        out = jnp.dot(x, weight_ref[...], preferred_element_type=jnp.float32)
        out = out.reshape(STEP, span, 3 * lanes)
        out = (
            out[:, :columns, :lanes]
            + out[:, STEP : STEP + columns, lanes : 2 * lanes]
            + out[:, 2 * STEP :, 2 * lanes :]
        )
        pred_ref[at[0]] = out[:, :, :channels]
        pred_ref[at[1]] = out[:, :, channels:]
        for h in range(2):
            pred_copy(n, h).start()
        cot = jnp.concatenate([cot_ref[at[h]].astype(jnp.float32) for h in range(2)], axis=2)
        zero = jnp.zeros((STEP, STEP, lanes), jnp.float32)
        shifted = [
            jnp.concatenate([zero] * b + [cot] + [zero] * (2 - b), axis=1).astype(jnp.bfloat16)
            for b in range(3)
        ]
        y = jnp.concatenate(shifted, axis=2).reshape(STEP * span, 3 * lanes)
        product_ref[...] += lax.dot_general(
            x, y, (((0,), (0,)), ((), ())), preferred_element_type=jnp.float32
        )
        back = lax.dot_general(
            y, weight_ref[...], (((1,), (1,)), ((), ())), preferred_element_type=jnp.float32
        ).reshape(STEP, span, 3 * lanes)
        for a in range(3):
            grad_ref[n + a] += back[:, :, a * lanes : (a + 1) * lanes]
        return carry

    lax.fori_loop(0, blocks, convolve, 0)

    def reduce(m, carry):
        u_total, v_total = carry
        at = pl.ds(pl.multiple_of(m * STEP, STEP), STEP)
        grad = grad_ref[m] * slope_ref[m]
        u_sum_ref[at] = jnp.sum(grad * u_col[None], axis=1)
        v_sum_ref[at] = jnp.sum(grad, axis=1)
        u_total = u_total + jnp.sum(grad * u_row_ref[at][:, None, :], axis=0)
        return u_total, v_total + jnp.sum(grad, axis=0)

    nothing = jnp.zeros((span, lanes), jnp.float32)
    u_total, v_total = lax.fori_loop(0, blocks + 2, reduce, (nothing, nothing))

    bins_ref[...] = jnp.zeros_like(bins_ref)
    u_sum, v_sum = u_sum_ref[...], v_sum_ref[...]
    at = pl.ds(pl.multiple_of(row0, STEP), depth)
    bins_ref[at] += jnp.where(in_first, u_sum, swap(v_sum))
    at = pl.ds(pl.multiple_of(row0 + half, STEP), depth)
    bins_ref[at] += jnp.where(in_first, swap(u_sum), v_sum)
    at = pl.ds(pl.multiple_of(col0, STEP), span)
    bins_ref[at] += jnp.where(in_first_col, u_total + swap(u_total), v_total + swap(v_total))

    for a in range(3):
        for b in range(3):
            block = product_ref[a * lanes : (a + 1) * lanes, b * lanes : (b + 1) * lanes]
            tap = (3 * a + b) * channels
            flat_ref[tap : tap + channels] = block[:channels, :channels] + block[channels:, channels:]
    taps = 9 * channels // 2
    packed_ref[...] = jnp.zeros_like(packed_ref)
    packed_ref[:taps] = jnp.concatenate([flat_ref[:taps], flat_ref[taps:]], axis=1)
    for r in range(n_row):
        part_ref[r, :chunk] = packed_ref[r * chunk : (r + 1) * chunk]
        part_ref[r, chunk:] = bins_ref[STEP + r * rows : STEP + (r + 1) * rows]

    for n in range(blocks):
        for h in range(2):
            pred_copy(n, h).wait()


def total_kernel(
    n_row,
    n_col,
    chunk,
    piece,
    part_ref,
    taps_ref,
    bins_ref,
    from_row,
    partial,
    from_col,
    total,
    every,
    send_a,
    recv_a,
    send_b,
    recv_b,
    send_c,
    recv_c,
    send_d,
    recv_d,
):
    row, col = lax.axis_index("row"), lax.axis_index("col")
    size = part_ref.shape[1]
    row_peers = [lax.rem(row + d, n_row) for d in range(1, n_row)]
    col_peers = [lax.rem(col + d, n_col) for d in range(1, n_col)]
    barrier = pltpu.get_barrier_semaphore()
    for peer in row_peers:
        signal(barrier, peer, col)
    for peer in col_peers:
        signal(barrier, row, peer)
    pl.semaphore_wait(barrier, n_row + n_col - 2)

    copies = []
    for d, peer in enumerate(row_peers):
        copy = remote(
            part_ref.at[peer], from_row.at[d], send_a.at[d], recv_a.at[d], peer, col
        )
        copy.start()
        copies.append(copy)
    if n_col * piece > size:
        partial[size:] = jnp.zeros((n_col * piece - size, partial.shape[1]), jnp.float32)
    for copy in copies:
        copy.wait()
    mine = part_ref[row]
    for d in range(n_row - 1):
        mine = mine + from_row[d]
    partial[:size] = mine

    def rows_of(owner):
        return pl.ds(pl.multiple_of(owner * piece, STEP), piece)

    copies = []
    for d, peer in enumerate(col_peers):
        copy = remote(
            partial.at[rows_of(peer)], from_col.at[d], send_b.at[d], recv_b.at[d], row, peer
        )
        copy.start()
        copies.append(copy)
    for copy in copies:
        copy.wait()
    mine = partial[rows_of(col)]
    for d in range(n_col - 1):
        mine = mine + from_col[d]
    total[rows_of(col)] = mine

    copies = []
    for d, peer in enumerate(col_peers):
        copy = remote(
            total.at[rows_of(col)], total.at[rows_of(col)], send_c.at[d], recv_c.at[d], row, peer
        )
        copy.start()
        copies.append(copy)
    for copy in copies:
        copy.wait()

    here = pl.ds(pl.multiple_of(row * chunk, STEP), chunk)
    every[here] = total[:chunk]
    copies = []
    for d, peer in enumerate(row_peers):
        copy = remote(
            total.at[pl.ds(0, chunk)], every.at[here], send_d.at[d], recv_d.at[d], peer, col
        )
        copy.start()
        copies.append(copy)
    bins_ref[...] = total[chunk:size]
    for copy in copies:
        copy.wait()
    taps, channels = taps_ref.shape
    taps_ref[: taps // 2] = every[: taps // 2, :channels]
    taps_ref[taps // 2 :] = every[: taps // 2, channels:]


def round_up(value, step):
    return -(-value // step) * step


def on_device(n_row, n_col, embedding, kernel, cotangent):
    rows, columns, channels = cotangent.shape
    lanes = 2 * channels
    bins = n_row * rows
    half = rows // 2
    blocks = half // STEP
    span = columns + 2 * STEP
    depth = half + 2 * STEP
    f32, bf16 = jnp.float32, jnp.bfloat16
    dma = pltpu.SemaphoreType.DMA
    wide = pl.pallas_call(
        functools.partial(gather_kernel, n_row),
        out_shape=jax.ShapeDtypeStruct((bins + 2 * STEP, lanes), f32),
        in_specs=[VMEM],
        out_specs=VMEM,
        scratch_shapes=[
            pltpu.VMEM((n_row - 1, rows, lanes), bf16),
            dma((n_row - 1,)),
            dma((n_row - 1,)),
        ],
        compiler_params=pltpu.CompilerParams(collective_id=0, has_side_effects=True),
        name="gather_embeddings",
    )(embedding)

    taps = 9 * channels
    chunk = round_up(-(-taps // (2 * n_row)), STEP)
    size = chunk + rows
    piece = round_up(-(-size // n_col), STEP)
    prediction, part = pl.pallas_call(
        functools.partial(tile_kernel, n_row, chunk),
        out_shape=(
            jax.ShapeDtypeStruct((rows, columns, channels), f32),
            jax.ShapeDtypeStruct((n_row, size, lanes), f32),
        ),
        in_specs=[VMEM, VMEM, ANY],
        out_specs=(ANY, VMEM),
        scratch_shapes=[
            pltpu.VMEM((rows, columns, channels), bf16),
            pltpu.VMEM((rows, columns, channels), f32),
            pltpu.VMEM((3 * lanes, 3 * lanes), bf16),
            pltpu.VMEM((depth, lanes), f32),
            pltpu.VMEM((depth, lanes), f32),
            pltpu.VMEM((blocks + 2, STEP * span, lanes), bf16),
            pltpu.VMEM((blocks + 2, STEP, span, lanes), f32),
            pltpu.VMEM((blocks + 2, STEP, span, lanes), f32),
            pltpu.VMEM((3 * lanes, 3 * lanes), f32),
            pltpu.VMEM((depth, lanes), f32),
            pltpu.VMEM((depth, lanes), f32),
            pltpu.VMEM((bins + 2 * STEP, lanes), f32),
            pltpu.VMEM((taps, channels), f32),
            pltpu.VMEM((n_row * chunk, lanes), f32),
            dma((blocks, 2)),
            dma((blocks, 2)),
        ],
        compiler_params=pltpu.CompilerParams(vmem_limit_bytes=48 * 2**20),
        name="tile_gradients",
    )(wide, kernel, cotangent)

    grad_kernel, grad_bins = pl.pallas_call(
        functools.partial(total_kernel, n_row, n_col, chunk, piece),
        out_shape=(
            jax.ShapeDtypeStruct((taps, channels), f32),
            jax.ShapeDtypeStruct((rows, lanes), f32),
        ),
        in_specs=[VMEM],
        out_specs=(VMEM, VMEM),
        scratch_shapes=[
            pltpu.VMEM((n_row - 1, size, lanes), f32),
            pltpu.VMEM((n_col * piece, lanes), f32),
            pltpu.VMEM((n_col - 1, piece, lanes), f32),
            pltpu.VMEM((n_col * piece, lanes), f32),
            pltpu.VMEM((n_row * chunk, lanes), f32),
        ]
        + [dma((n_row - 1,))] * 2
        + [dma((n_col - 1,))] * 4
        + [dma((n_row - 1,))] * 2,
        compiler_params=pltpu.CompilerParams(
            collective_id=1, has_side_effects=True, vmem_limit_bytes=32 * 2**20
        ),
        name="sum_gradients",
    )(part)
    return (
        prediction,
        grad_kernel.reshape(kernel.shape) / bins,
        grad_bins * float(bins) ** (-0.5),
    )


def solution(mesh):
    in_specs = (P("row", None), P(), P("row", "col", None))
    out_specs = (P("row", "col", None), P(), P("row", None))
    return jax.shard_map(
        functools.partial(on_device, mesh.shape["row"], mesh.shape["col"]),
        mesh=mesh,
        in_specs=in_specs,
        out_specs=out_specs,
        check_vma=False,
    )
```

```python
import functools

import jax
import jax.numpy as jnp
from jax import lax
from jax.experimental import pallas as pl
from jax.experimental.pallas import tpu as pltpu
from jax.sharding import PartitionSpec as P

STEP = 8
MESH = pl.DeviceIdType.MESH
VMEM = pl.BlockSpec(memory_space=pltpu.VMEM)
ANY = pl.BlockSpec(memory_space=pl.ANY)


def signal(barrier, row, col):
    pl.semaphore_signal(barrier, inc=1, device_id=(row, col), device_id_type=MESH)


def remote(src, dst, send, recv, row, col):
    return pltpu.make_async_remote_copy(
        src_ref=src,
        dst_ref=dst,
        send_sem=send,
        recv_sem=recv,
        device_id=(row, col),
        device_id_type=MESH,
    )


def gather_kernel(n_row, emb_ref, out_ref, held, send_sem, recv_sem):
    row, col = lax.axis_index("row"), lax.axis_index("col")
    rows = emb_ref.shape[0]
    barrier = pltpu.get_barrier_semaphore()
    peers = [lax.rem(row + d, n_row) for d in range(1, n_row)]
    for peer in peers:
        signal(barrier, peer, col)
    pl.semaphore_wait(barrier, n_row - 1)
    copies = []
    for d, peer in enumerate(peers):
        copy = remote(emb_ref, held.at[d], send_sem.at[d], recv_sem.at[d], peer, col)
        copy.start()
        copies.append(copy)
    border = jnp.zeros((STEP, out_ref.shape[1]), jnp.float32)
    out_ref[:STEP] = border
    out_ref[STEP + n_row * rows :] = border
    out_ref[pl.ds(pl.multiple_of(STEP + row * rows, STEP), rows)] = emb_ref[...].astype(jnp.float32)
    for d, copy in enumerate(copies):
        copy.wait()
        owner = lax.rem(row + n_row - 1 - d, n_row)
        out_ref[pl.ds(pl.multiple_of(STEP + owner * rows, STEP), rows)] = held[d].astype(
            jnp.float32
        )


def tile_kernel(
    wide_ref,
    kernel_ref,
    cot_hbm,
    pred_hbm,
    packed_ref,
    row_ref,
    col_ref,
    cot_ref,
    pred_ref,
    weight_ref,
    u_col_ref,
    v_col_ref,
    act_ref,
    slope_ref,
    grad_ref,
    product_ref,
    u_sum_ref,
    v_sum_ref,
    flat_ref,
    cot_sem,
    pred_sem,
):
    columns, channels, rows = cot_ref.shape
    half = columns // 2
    blocks = half // STEP
    span = rows + 2 * STEP
    lanes = 2 * channels
    bins = wide_ref.shape[0] - 2 * STEP
    row0 = lax.axis_index("row") * rows
    col0 = lax.axis_index("col") * columns

    def cot_copy(n, h):
        at = pl.ds(h * half + n * STEP, STEP)
        return pltpu.make_async_copy(cot_hbm.at[at], cot_ref.at[at], cot_sem.at[n, h])

    def pred_copy(n, h):
        at = pl.ds(h * half + n * STEP, STEP)
        return pltpu.make_async_copy(pred_ref.at[at], pred_hbm.at[at], pred_sem.at[n, h])

    for n in range(blocks):
        for h in range(2):
            cot_copy(n, h).start()

    none = jnp.zeros((channels, channels), jnp.float32)
    for a in range(3):
        for b in range(3):
            w = kernel_ref[a, b].astype(jnp.float32)
            both = jnp.concatenate(
                [jnp.concatenate([w, none], axis=1), jnp.concatenate([none, w], axis=1)], axis=0
            )
            weight_ref[b * lanes : (b + 1) * lanes, a * lanes : (a + 1) * lanes] = both.astype(
                jnp.bfloat16
            )

    def first(shape):
        return lax.broadcasted_iota(jnp.int32, shape, len(shape) - 1) < channels

    def swap(x):
        return pltpu.roll(x, channels, 1)

    depth = half + 2 * STEP
    low = wide_ref[pl.ds(pl.multiple_of(col0, STEP), depth)]
    high = wide_ref[pl.ds(pl.multiple_of(col0 + half, STEP), depth)]
    in_first = first((depth, lanes))
    u_col_ref[...] = jnp.where(in_first, low, swap(high))
    v_col_ref[...] = jnp.where(in_first, swap(low), high)
    side = wide_ref[pl.ds(pl.multiple_of(row0, STEP), span)]
    in_first_row = first((span, lanes))
    u_row = jnp.where(in_first_row, side, swap(side))
    v_row = jnp.where(in_first_row, swap(side), side)
    row_pos = row0 - STEP + lax.broadcasted_iota(jnp.int32, (span, lanes), 0)
    row_in = jnp.where((row_pos >= 0) & (row_pos < bins), 1.0, 0.0)

    def activate(m, carry):
        at = pl.ds(pl.multiple_of(m * STEP, STEP), STEP)
        shape = (STEP, 1, lanes)
        pos = col0 - STEP + m * STEP + lax.broadcasted_iota(jnp.int32, shape, 0)
        pos = pos + jnp.where(first(shape), 0, half)
        col_in = jnp.where((pos >= 0) & (pos < bins), 1.0, 0.0)
        pairs = u_col_ref[at][:, None, :] * u_row[None] + v_col_ref[at][:, None, :] + v_row[None]
        s = 0.5 * jnp.tanh(0.5 * pairs) + 0.5
        s = s * (col_in * row_in[None])
        act = pairs * s
        act_ref[m] = act.reshape(STEP * span, lanes).astype(jnp.bfloat16)
        slope_ref[m] = s + act * (1.0 - s)
        grad_ref[m] = jnp.zeros((STEP, span, lanes), jnp.float32)
        return carry

    lax.fori_loop(0, blocks + 2, activate, 0)
    product_ref[...] = jnp.zeros_like(product_ref)

    def convolve(n, carry):
        for h in range(2):
            cot_copy(n, h).wait()
        x = jnp.concatenate([act_ref[n + b] for b in range(3)], axis=1)
        out = jnp.dot(x, weight_ref[...], preferred_element_type=jnp.float32)
        out = out.reshape(STEP, span, 3 * lanes)
        out = (
            out[:, :rows, :lanes]
            + out[:, STEP : STEP + rows, lanes : 2 * lanes]
            + out[:, 2 * STEP :, 2 * lanes :]
        )
        cot = []
        for k in range(STEP):
            at = n * STEP + k
            turned = out[k].T
            pred_ref[at] = turned[:channels]
            pred_ref[half + at] = turned[channels:]
            stack = jnp.concatenate([cot_ref[at], cot_ref[half + at]], axis=0)
            cot.append(stack.astype(jnp.float32).T)
        for h in range(2):
            pred_copy(n, h).start()
        cot = jnp.stack(cot)
        zero = jnp.zeros((STEP, STEP, lanes), jnp.float32)
        shifted = [
            jnp.concatenate([zero] * a + [cot] + [zero] * (2 - a), axis=1).astype(jnp.bfloat16)
            for a in range(3)
        ]
        y = jnp.concatenate(shifted, axis=2).reshape(STEP * span, 3 * lanes)
        product_ref[...] += lax.dot_general(
            x, y, (((0,), (0,)), ((), ())), preferred_element_type=jnp.float32
        )
        back = lax.dot_general(
            y, weight_ref[...], (((1,), (1,)), ((), ())), preferred_element_type=jnp.float32
        ).reshape(STEP, span, 3 * lanes)
        for b in range(3):
            grad_ref[n + b] += back[:, :, b * lanes : (b + 1) * lanes]
        return carry

    lax.fori_loop(0, blocks, convolve, 0)

    def reduce(m, carry):
        u_total, v_total = carry
        at = pl.ds(pl.multiple_of(m * STEP, STEP), STEP)
        grad = grad_ref[m] * slope_ref[m]
        u_sum_ref[at] = jnp.sum(grad * u_row[None], axis=1)
        v_sum_ref[at] = jnp.sum(grad, axis=1)
        u_total = u_total + jnp.sum(grad * u_col_ref[at][:, None, :], axis=0)
        return u_total, v_total + jnp.sum(grad, axis=0)

    nothing = jnp.zeros((span, lanes), jnp.float32)
    u_total, v_total = lax.fori_loop(0, blocks + 2, reduce, (nothing, nothing))

    row_ref[...] = jnp.where(in_first_row, u_total + swap(u_total), v_total + swap(v_total))
    u_sum, v_sum = u_sum_ref[...], v_sum_ref[...]
    col_ref[:depth] = jnp.where(in_first, u_sum, swap(v_sum))
    col_ref[depth:] = jnp.zeros((half, lanes), jnp.float32)
    col_ref[half:] += jnp.where(in_first, swap(u_sum), v_sum)

    for a in range(3):
        for b in range(3):
            block = product_ref[b * lanes : (b + 1) * lanes, a * lanes : (a + 1) * lanes]
            tap = (3 * a + b) * channels
            flat_ref[tap : tap + channels] = block[:channels, :channels] + block[channels:, channels:]
    taps = 9 * channels // 2
    packed_ref[:taps] = jnp.concatenate([flat_ref[:taps], flat_ref[taps:]], axis=1)
    if packed_ref.shape[0] > taps:
        packed_ref[taps:] = jnp.zeros((packed_ref.shape[0] - taps, lanes), jnp.float32)

    for n in range(blocks):
        for h in range(2):
            pred_copy(n, h).wait()


def total_kernel(
    n_row,
    n_col,
    chunk,
    piece,
    columns,
    packed_ref,
    row_ref,
    col_ref,
    taps_ref,
    bins_ref,
    from_row,
    from_owned,
    partial,
    from_col,
    total,
    every,
    border,
    send_a,
    recv_a,
    send_b,
    recv_b,
    send_c,
    recv_c,
    send_d,
    recv_d,
    send_e,
    recv_e,
    send_f,
    recv_f,
):
    row, col = lax.axis_index("row"), lax.axis_index("col")
    span = row_ref.shape[0]
    rows = span - 2 * STEP
    size = chunk + span
    ratio = rows // columns
    owner = col // ratio
    row_peers = [lax.rem(row + d, n_row) for d in range(1, n_row)]
    col_peers = [lax.rem(col + d, n_col) for d in range(1, n_col)]
    barrier = pltpu.get_barrier_semaphore()
    for peer in row_peers:
        signal(barrier, peer, col)
    for peer in col_peers:
        signal(barrier, row, peer)
    pl.semaphore_wait(barrier, n_row + n_col - 2)

    def rows_at(index, count):
        return pl.ds(pl.multiple_of(index * count, STEP), count)

    away = lax.rem(owner + n_row - row, n_row) - 1

    def owned_copy(d, target):
        return remote(col_ref, from_owned.at[d], send_e.at[0], recv_e.at[d], target, col)

    @pl.when(row != owner)
    def _():
        owned_copy(away, owner).start()

    copies = []
    for d, peer in enumerate(row_peers):
        copy = remote(
            packed_ref.at[rows_at(peer, chunk)],
            from_row.at[d],
            send_a.at[d],
            recv_a.at[d],
            peer,
            col,
        )
        copy.start()
        copies.append(copy)
    if n_col * piece > size:
        partial[size:] = jnp.zeros((n_col * piece - size, partial.shape[1]), jnp.float32)
    partial[chunk:size] = row_ref[...]

    @pl.when(row == owner)
    def _():
        mine = col_ref[...]
        for d in range(n_row - 1):
            owned_copy(d, row_peers[0]).wait_recv()
            mine = mine + from_owned[d]
        start = chunk + lax.rem(col, ratio) * columns
        partial[pl.ds(pl.multiple_of(start, STEP), columns + 2 * STEP)] += mine

    @pl.when(row != owner)
    def _():
        owned_copy(away, owner).wait_send()

    for copy in copies:
        copy.wait()
    mine = packed_ref[rows_at(row, chunk)]
    for d in range(n_row - 1):
        mine = mine + from_row[d]
    partial[:chunk] = mine

    copies = []
    for d, peer in enumerate(col_peers):
        copy = remote(
            partial.at[rows_at(peer, piece)], from_col.at[d], send_b.at[d], recv_b.at[d], row, peer
        )
        copy.start()
        copies.append(copy)
    for copy in copies:
        copy.wait()
    mine = partial[rows_at(col, piece)]
    for d in range(n_col - 1):
        mine = mine + from_col[d]
    here = rows_at(col, piece)
    total[here] = mine

    copies = []
    for d, peer in enumerate(col_peers):
        copy = remote(total.at[here], total.at[here], send_c.at[d], recv_c.at[d], row, peer)
        copy.start()
        copies.append(copy)
    for copy in copies:
        copy.wait()

    below, above = lax.rem(row + n_row - 1, n_row), lax.rem(row + 1, n_row)
    copies = []
    for d, (peer, start) in enumerate([(below, chunk), (above, size - STEP)]):
        copy = remote(
            total.at[pl.ds(start, STEP)], border.at[d], send_f.at[d], recv_f.at[d], peer, col
        )
        copy.start()
        copies.append(copy)
    here = rows_at(row, chunk)
    for d, peer in enumerate(row_peers):
        copy = remote(
            total.at[pl.ds(0, chunk)], every.at[here], send_d.at[d], recv_d.at[d], peer, col
        )
        copy.start()
        copies.append(copy)
    every[here] = total[:chunk]
    bins_ref[...] = total[chunk + STEP : size - STEP]
    for copy in copies:
        copy.wait()
    bins_ref[rows - STEP :] += border[0]
    bins_ref[:STEP] += border[1]
    taps, channels = taps_ref.shape
    taps_ref[: taps // 2] = every[: taps // 2, :channels]
    taps_ref[taps // 2 :] = every[: taps // 2, channels:]


def round_up(value, step):
    return -(-value // step) * step


def on_device(n_row, n_col, embedding, kernel, cotangent):
    rows, columns, channels = cotangent.shape
    lanes = 2 * channels
    bins = n_row * rows
    half = columns // 2
    blocks = half // STEP
    span = rows + 2 * STEP
    depth = half + 2 * STEP
    f32, bf16 = jnp.float32, jnp.bfloat16
    dma = pltpu.SemaphoreType.DMA
    wide = pl.pallas_call(
        functools.partial(gather_kernel, n_row),
        out_shape=jax.ShapeDtypeStruct((bins + 2 * STEP, lanes), f32),
        in_specs=[VMEM],
        out_specs=VMEM,
        scratch_shapes=[
            pltpu.VMEM((n_row - 1, rows, lanes), bf16),
            dma((n_row - 1,)),
            dma((n_row - 1,)),
        ],
        compiler_params=pltpu.CompilerParams(collective_id=0, has_side_effects=True),
        name="gather_embeddings",
    )(embedding)

    taps = 9 * channels
    chunk = round_up(-(-taps // (2 * n_row)), STEP)
    size = chunk + span
    piece = round_up(-(-size // n_col), STEP)
    prediction, packed, row_part, col_part = pl.pallas_call(
        tile_kernel,
        out_shape=(
            jax.ShapeDtypeStruct((columns, channels, rows), f32),
            jax.ShapeDtypeStruct((n_row * chunk, lanes), f32),
            jax.ShapeDtypeStruct((span, lanes), f32),
            jax.ShapeDtypeStruct((columns + 2 * STEP, lanes), f32),
        ),
        in_specs=[VMEM, VMEM, ANY],
        out_specs=(ANY, VMEM, VMEM, VMEM),
        scratch_shapes=[
            pltpu.VMEM((columns, channels, rows), bf16),
            pltpu.VMEM((columns, channels, rows), f32),
            pltpu.VMEM((3 * lanes, 3 * lanes), bf16),
            pltpu.VMEM((depth, lanes), f32),
            pltpu.VMEM((depth, lanes), f32),
            pltpu.VMEM((blocks + 2, STEP * span, lanes), bf16),
            pltpu.VMEM((blocks + 2, STEP, span, lanes), f32),
            pltpu.VMEM((blocks + 2, STEP, span, lanes), f32),
            pltpu.VMEM((3 * lanes, 3 * lanes), f32),
            pltpu.VMEM((depth, lanes), f32),
            pltpu.VMEM((depth, lanes), f32),
            pltpu.VMEM((taps, channels), f32),
            dma((blocks, 2)),
            dma((blocks, 2)),
        ],
        compiler_params=pltpu.CompilerParams(vmem_limit_bytes=48 * 2**20),
        name="tile_gradients",
    )(wide, kernel, cotangent.transpose(1, 2, 0))

    grad_kernel, grad_bins = pl.pallas_call(
        functools.partial(total_kernel, n_row, n_col, chunk, piece, columns),
        out_shape=(
            jax.ShapeDtypeStruct((taps, channels), f32),
            jax.ShapeDtypeStruct((rows, lanes), f32),
        ),
        in_specs=[VMEM, VMEM, VMEM],
        out_specs=(VMEM, VMEM),
        scratch_shapes=[
            pltpu.VMEM((n_row - 1, chunk, lanes), f32),
            pltpu.VMEM((n_row - 1, columns + 2 * STEP, lanes), f32),
            pltpu.VMEM((n_col * piece, lanes), f32),
            pltpu.VMEM((n_col - 1, piece, lanes), f32),
            pltpu.VMEM((n_col * piece, lanes), f32),
            pltpu.VMEM((n_row * chunk, lanes), f32),
            pltpu.VMEM((2, STEP, lanes), f32),
        ]
        + [dma((n_row - 1,))] * 2
        + [dma((n_col - 1,))] * 4
        + [dma((n_row - 1,))] * 2
        + [dma((1,)), dma((n_row - 1,)), dma((2,)), dma((2,))],
        compiler_params=pltpu.CompilerParams(
            collective_id=1, has_side_effects=True, vmem_limit_bytes=32 * 2**20
        ),
        name="sum_gradients",
    )(packed, row_part, col_part)
    return (
        prediction.transpose(2, 0, 1),
        grad_kernel.reshape(kernel.shape) / bins,
        grad_bins * float(bins) ** (-0.5),
    )


def solution(mesh):
    in_specs = (P("row", None), P(), P("row", "col", None))
    out_specs = (P("row", "col", None), P(), P("row", None))
    return jax.shard_map(
        functools.partial(on_device, mesh.shape["row"], mesh.shape["col"]),
        mesh=mesh,
        in_specs=in_specs,
        out_specs=out_specs,
        check_vma=False,
    )
```

```python
import functools
import types

import jax
import jax.numpy as jnp
from jax import lax
from jax.experimental import pallas as pl
from jax.experimental.pallas import tpu as pltpu
from jax.sharding import PartitionSpec as P

STEP = 8
MESH = pl.DeviceIdType.MESH
VMEM = pl.BlockSpec(memory_space=pltpu.VMEM)
ANY = pl.BlockSpec(memory_space=pl.ANY)


def signal(barrier, row, col):
    pl.semaphore_signal(barrier, inc=1, device_id=(row, col), device_id_type=MESH)


def remote(src, dst, send, recv, row, col):
    return pltpu.make_async_remote_copy(
        src_ref=src,
        dst_ref=dst,
        send_sem=send,
        recv_sem=recv,
        device_id=(row, col),
        device_id_type=MESH,
    )


def tile_kernel(n_row, n_col, chunk, piece, refs):
    emb_hbm, kernel_hbm, cot_hbm = refs.emb_hbm, refs.kernel_hbm, refs.cot_hbm
    wide_ref, weight_ref, cot_ref, pred_ref = refs.wide, refs.weight, refs.cot, refs.pred
    act_ref, turned_ref, grad_ref, product_ref = refs.act, refs.turned, refs.grad, refs.product
    col_ref, partial, total, every = refs.col, refs.partial, refs.total, refs.every
    columns, channels, rows = cot_ref.shape
    half = columns // 2
    blocks = half // STEP
    span = rows + 2 * STEP
    depth = half + 2 * STEP
    lanes = 2 * channels
    bins = n_row * rows
    size = chunk + span
    ratio = rows // columns
    row, col = lax.axis_index("row"), lax.axis_index("col")
    row0, col0 = row * rows, col * columns
    owner = col // ratio
    row_peers = [lax.rem(row + d, n_row) for d in range(1, n_row)]
    col_peers = [lax.rem(col + d, n_col) for d in range(1, n_col)]

    def local(source, target, sem):
        return pltpu.make_async_copy(source, target, sem)

    def cot_copy(n, h):
        at = pl.ds(h * half + n * STEP, STEP)
        return local(cot_hbm.at[at], cot_ref.at[at], refs.cot_sem.at[n, h])

    def pred_copy(n, h):
        at = pl.ds(h * half + n * STEP, STEP)
        return local(pred_ref.at[at], refs.pred_hbm.at[at], refs.pred_sem.at[n, h])

    def rows_at(index, count):
        return pl.ds(pl.multiple_of(index * count, STEP), count)

    def start(copies):
        for copy in copies:
            copy.start()

    def wait(copies):
        for copy in copies:
            copy.wait()

    barrier = pltpu.get_barrier_semaphore()
    for peer in row_peers:
        signal(barrier, peer, col)
    for peer in col_peers:
        signal(barrier, row, peer)
    inputs = [
        local(emb_hbm, refs.emb, refs.in_sem.at[0]),
        local(kernel_hbm, refs.kernel, refs.in_sem.at[1]),
    ]
    start(inputs)
    start([cot_copy(n, h) for n in range(blocks) for h in range(2)])

    grad_ref[...] = jnp.zeros_like(grad_ref)
    product_ref[...] = jnp.zeros_like(product_ref)
    zeros = jnp.zeros((STEP, lanes), jnp.float32)
    wide_ref[:STEP] = zeros
    wide_ref[STEP + bins :] = zeros
    if n_col * piece > size:
        partial[size:] = jnp.zeros((n_col * piece - size, lanes), jnp.float32)

    wait(inputs)
    pl.semaphore_wait(barrier, n_row + n_col - 2)
    gather = [
        remote(refs.emb, refs.held.at[d], refs.send_g.at[d], refs.recv_g.at[d], peer, col)
        for d, peer in enumerate(row_peers)
    ]
    start(gather)

    none = jnp.zeros((channels, channels), jnp.float32)
    for a in range(3):
        for b in range(3):
            w = refs.kernel[a, b].astype(jnp.float32)
            both = jnp.concatenate(
                [jnp.concatenate([w, none], axis=1), jnp.concatenate([none, w], axis=1)], axis=0
            )
            weight_ref[b * lanes : (b + 1) * lanes, a * lanes : (a + 1) * lanes] = both.astype(
                jnp.bfloat16
            )

    def spread(n, carry):
        wait([cot_copy(n, h) for h in range(2)])
        cot = []
        for k in range(STEP):
            at = n * STEP + k
            stack = jnp.concatenate([cot_ref[at], cot_ref[half + at]], axis=0)
            cot.append(stack.astype(jnp.float32).T)
        cot = jnp.stack(cot)
        zero = jnp.zeros((STEP, STEP, lanes), jnp.float32)
        shifted = [
            jnp.concatenate([zero] * a + [cot] + [zero] * (2 - a), axis=1).astype(jnp.bfloat16)
            for a in range(3)
        ]
        y = jnp.concatenate(shifted, axis=2).reshape(STEP * span, 3 * lanes)
        turned_ref[n] = y
        back = lax.dot_general(
            y, weight_ref[...], (((1,), (1,)), ((), ())), preferred_element_type=jnp.float32
        ).reshape(STEP, span, 3 * lanes)
        for b in range(3):
            grad_ref[n + b] += back[:, :, b * lanes : (b + 1) * lanes]
        return carry

    lax.fori_loop(0, blocks, spread, 0)

    wide_ref[pl.ds(pl.multiple_of(STEP + row0, STEP), rows)] = refs.emb[...].astype(jnp.float32)
    for d, copy in enumerate(gather):
        copy.wait()
        peer = lax.rem(row + n_row - 1 - d, n_row)
        at = pl.ds(pl.multiple_of(STEP + peer * rows, STEP), rows)
        wide_ref[at] = refs.held[d].astype(jnp.float32)

    def first(shape):
        return lax.broadcasted_iota(jnp.int32, shape, len(shape) - 1) < channels

    def swap(x):
        return pltpu.roll(x, channels, 1)

    low = wide_ref[pl.ds(pl.multiple_of(col0, STEP), depth)]
    high = wide_ref[pl.ds(pl.multiple_of(col0 + half, STEP), depth)]
    in_first = first((depth, lanes))
    refs.u_col[...] = jnp.where(in_first, low, swap(high))
    refs.v_col[...] = jnp.where(in_first, swap(low), high)
    side = wide_ref[pl.ds(pl.multiple_of(row0, STEP), span)]
    in_first_row = first((span, lanes))
    u_row = jnp.where(in_first_row, side, swap(side))
    v_row = jnp.where(in_first_row, swap(side), side)
    row_pos = row0 - STEP + lax.broadcasted_iota(jnp.int32, (span, lanes), 0)
    row_in = jnp.where((row_pos >= 0) & (row_pos < bins), 1.0, 0.0)

    def activate(m, carry):
        u_total, v_total = carry
        at = pl.ds(pl.multiple_of(m * STEP, STEP), STEP)
        shape = (STEP, 1, lanes)
        pos = col0 - STEP + m * STEP + lax.broadcasted_iota(jnp.int32, shape, 0)
        pos = pos + jnp.where(first(shape), 0, half)
        col_in = jnp.where((pos >= 0) & (pos < bins), 1.0, 0.0)
        u_col = refs.u_col[at][:, None, :]
        pairs = u_col * u_row[None] + refs.v_col[at][:, None, :] + v_row[None]
        s = 0.5 * jnp.tanh(0.5 * pairs) + 0.5
        s = s * (col_in * row_in[None])
        act = pairs * s
        act_ref[m] = act.reshape(STEP * span, lanes).astype(jnp.bfloat16)
        grad = grad_ref[m] * (s + act * (1.0 - s))
        refs.u_sum[at] = jnp.sum(grad * u_row[None], axis=1)
        refs.v_sum[at] = jnp.sum(grad, axis=1)
        u_total = u_total + jnp.sum(grad * u_col, axis=0)
        return u_total, v_total + jnp.sum(grad, axis=0)

    nothing = jnp.zeros((span, lanes), jnp.float32)
    u_total, v_total = lax.fori_loop(0, blocks + 2, activate, (nothing, nothing))

    row_part = jnp.where(in_first_row, u_total + swap(u_total), v_total + swap(v_total))
    partial[chunk:size] = row_part
    u_sum, v_sum = refs.u_sum[...], refs.v_sum[...]
    col_ref[:depth] = jnp.where(in_first, u_sum, swap(v_sum))
    col_ref[depth:] = jnp.zeros((half, lanes), jnp.float32)
    col_ref[half:] += jnp.where(in_first, swap(u_sum), v_sum)

    away = lax.rem(owner + n_row - row, n_row) - 1

    def owned_copy(d, target):
        return remote(
            col_ref, refs.from_owned.at[d], refs.send_e.at[0], refs.recv_e.at[d], target, col
        )

    @pl.when(row != owner)
    def _():
        owned_copy(away, owner).start()

    def lay(n):
        return jnp.concatenate([act_ref[n + b] for b in range(3)], axis=1)

    def multiply(n, carry):
        product_ref[...] += lax.dot_general(
            lay(n), turned_ref[n], (((0,), (0,)), ((), ())), preferred_element_type=jnp.float32
        )
        return carry

    lax.fori_loop(0, blocks, multiply, 0)
    for a in range(3):
        for b in range(3):
            block = product_ref[b * lanes : (b + 1) * lanes, a * lanes : (a + 1) * lanes]
            tap = (3 * a + b) * channels
            refs.flat[tap : tap + channels] = (
                block[:channels, :channels] + block[channels:, channels:]
            )
    taps = 9 * channels // 2
    refs.packed[:taps] = jnp.concatenate([refs.flat[:taps], refs.flat[taps:]], axis=1)
    if n_row * chunk > taps:
        refs.packed[taps:] = jnp.zeros((n_row * chunk - taps, lanes), jnp.float32)
    to_row = [
        remote(
            refs.packed.at[rows_at(peer, chunk)],
            refs.from_row.at[d],
            refs.send_a.at[d],
            refs.recv_a.at[d],
            peer,
            col,
        )
        for d, peer in enumerate(row_peers)
    ]
    start(to_row)

    def predict(n, carry):
        out = jnp.dot(lay(n), weight_ref[...], preferred_element_type=jnp.float32)
        out = out.reshape(STEP, span, 3 * lanes)
        out = (
            out[:, :rows, :lanes]
            + out[:, STEP : STEP + rows, lanes : 2 * lanes]
            + out[:, 2 * STEP :, 2 * lanes :]
        )
        for k in range(STEP):
            at = n * STEP + k
            turned = out[k].T
            pred_ref[at] = turned[:channels]
            pred_ref[half + at] = turned[channels:]
        start([pred_copy(n, h) for h in range(2)])
        return carry

    bounds = [blocks * part // 4 for part in (0, 1, 2, 4)]
    lax.fori_loop(bounds[0], bounds[1], predict, 0)

    @pl.when(row == owner)
    def _():
        mine = col_ref[...]
        for d in range(n_row - 1):
            owned_copy(d, row_peers[0]).wait_recv()
            mine = mine + refs.from_owned[d]
        begin = chunk + lax.rem(col, ratio) * columns
        partial[pl.ds(pl.multiple_of(begin, STEP), columns + 2 * STEP)] += mine

    @pl.when(row != owner)
    def _():
        owned_copy(away, owner).wait_send()

    wait(to_row)
    mine = refs.packed[rows_at(row, chunk)]
    for d in range(n_row - 1):
        mine = mine + refs.from_row[d]
    partial[:chunk] = mine

    to_col = [
        remote(
            partial.at[rows_at(peer, piece)],
            refs.from_col.at[d],
            refs.send_b.at[d],
            refs.recv_b.at[d],
            row,
            peer,
        )
        for d, peer in enumerate(col_peers)
    ]
    start(to_col)
    lax.fori_loop(bounds[1], bounds[2], predict, 0)
    wait(to_col)
    here = rows_at(col, piece)
    mine = partial[here]
    for d in range(n_col - 1):
        mine = mine + refs.from_col[d]
    total[here] = mine

    back_col = [
        remote(total.at[here], total.at[here], refs.send_c.at[d], refs.recv_c.at[d], row, peer)
        for d, peer in enumerate(col_peers)
    ]
    start(back_col)
    lax.fori_loop(bounds[2], bounds[3], predict, 0)
    wait(back_col)

    below, above = lax.rem(row + n_row - 1, n_row), lax.rem(row + 1, n_row)
    here = rows_at(row, chunk)
    last = [
        remote(
            total.at[pl.ds(begin, STEP)],
            refs.border.at[d],
            refs.send_f.at[d],
            refs.recv_f.at[d],
            peer,
            col,
        )
        for d, (peer, begin) in enumerate([(below, chunk), (above, size - STEP)])
    ] + [
        remote(
            total.at[pl.ds(0, chunk)], every.at[here], refs.send_d.at[d], refs.recv_d.at[d], peer, col
        )
        for d, peer in enumerate(row_peers)
    ]
    start(last)
    every[here] = total[:chunk]
    refs.bins_out[...] = total[chunk + STEP : size - STEP]
    wait(last)
    refs.bins_out[rows - STEP :] += refs.border[0]
    refs.bins_out[:STEP] += refs.border[1]
    refs.taps_out[:taps] = every[:taps, :channels]
    refs.taps_out[taps:] = every[:taps, channels:]
    wait([pred_copy(n, h) for n in range(blocks) for h in range(2)])


def finish_kernel(bins, pred_in, taps_in, bins_in, pred_out, taps_out, bins_out, sem):
    parts = sem.shape[0]
    count = pred_in.shape[0] // parts
    copies = []
    for part in range(parts):
        at = pl.ds(part * count, count)
        copy = pltpu.make_async_copy(pred_in.at[at], pred_out.at[at], sem.at[part])
        copy.start()
        copies.append(copy)
    taps_out[...] = taps_in[...] / bins
    bins_out[...] = bins_in[...] * float(bins) ** (-0.5)
    for copy in copies:
        copy.wait()


def round_up(value, step):
    return -(-value // step) * step


def on_device(n_row, n_col, embedding, kernel, cotangent):
    rows, columns, channels = cotangent.shape
    lanes = 2 * channels
    bins = n_row * rows
    half = columns // 2
    blocks = half // STEP
    span = rows + 2 * STEP
    depth = half + 2 * STEP
    taps = 9 * channels
    chunk = round_up(-(-taps // (2 * n_row)), STEP)
    piece = round_up(-(-(chunk + span) // n_col), STEP)
    f32, bf16 = jnp.float32, jnp.bfloat16
    dma = pltpu.SemaphoreType.DMA
    outputs = {
        "pred_hbm": jax.ShapeDtypeStruct((columns, channels, rows), f32),
        "taps_out": jax.ShapeDtypeStruct((taps, channels), f32),
        "bins_out": jax.ShapeDtypeStruct((rows, lanes), f32),
    }
    scratch = {
        "emb": pltpu.VMEM((rows, lanes), bf16),
        "kernel": pltpu.VMEM(kernel.shape, bf16),
        "cot": pltpu.VMEM((columns, channels, rows), bf16),
        "pred": pltpu.VMEM((columns, channels, rows), f32),
        "held": pltpu.VMEM((n_row - 1, rows, lanes), bf16),
        "wide": pltpu.VMEM((bins + 2 * STEP, lanes), f32),
        "weight": pltpu.VMEM((3 * lanes, 3 * lanes), bf16),
        "u_col": pltpu.VMEM((depth, lanes), f32),
        "v_col": pltpu.VMEM((depth, lanes), f32),
        "act": pltpu.VMEM((blocks + 2, STEP * span, lanes), bf16),
        "turned": pltpu.VMEM((blocks, STEP * span, 3 * lanes), bf16),
        "grad": pltpu.VMEM((blocks + 2, STEP, span, lanes), f32),
        "product": pltpu.VMEM((3 * lanes, 3 * lanes), f32),
        "u_sum": pltpu.VMEM((depth, lanes), f32),
        "v_sum": pltpu.VMEM((depth, lanes), f32),
        "flat": pltpu.VMEM((taps, channels), f32),
        "packed": pltpu.VMEM((n_row * chunk, lanes), f32),
        "col": pltpu.VMEM((columns + 2 * STEP, lanes), f32),
        "from_row": pltpu.VMEM((n_row - 1, chunk, lanes), f32),
        "from_owned": pltpu.VMEM((n_row - 1, columns + 2 * STEP, lanes), f32),
        "partial": pltpu.VMEM((n_col * piece, lanes), f32),
        "from_col": pltpu.VMEM((n_col - 1, piece, lanes), f32),
        "total": pltpu.VMEM((n_col * piece, lanes), f32),
        "every": pltpu.VMEM((n_row * chunk, lanes), f32),
        "border": pltpu.VMEM((2, STEP, lanes), f32),
        "in_sem": dma((2,)),
        "cot_sem": dma((blocks, 2)),
        "pred_sem": dma((blocks, 2)),
        "send_g": dma((n_row - 1,)),
        "recv_g": dma((n_row - 1,)),
        "send_a": dma((n_row - 1,)),
        "recv_a": dma((n_row - 1,)),
        "send_b": dma((n_col - 1,)),
        "recv_b": dma((n_col - 1,)),
        "send_c": dma((n_col - 1,)),
        "recv_c": dma((n_col - 1,)),
        "send_d": dma((n_row - 1,)),
        "recv_d": dma((n_row - 1,)),
        "send_e": dma((1,)),
        "recv_e": dma((n_row - 1,)),
        "send_f": dma((2,)),
        "recv_f": dma((2,)),
    }
    names = ["emb_hbm", "kernel_hbm", "cot_hbm", *outputs, *scratch]

    def tile(*refs):
        tile_kernel(n_row, n_col, chunk, piece, types.SimpleNamespace(**dict(zip(names, refs))))

    prediction, grad_kernel, grad_bins = pl.pallas_call(
        tile,
        out_shape=tuple(outputs.values()),
        in_specs=[ANY, ANY, ANY],
        out_specs=(ANY, VMEM, VMEM),
        scratch_shapes=list(scratch.values()),
        compiler_params=pltpu.CompilerParams(
            collective_id=0, has_side_effects=True, vmem_limit_bytes=60 * 2**20
        ),
        name="tile_gradients",
    )(embedding, kernel, cotangent.transpose(1, 2, 0))

    prediction, grad_kernel, grad_bins = pl.pallas_call(
        functools.partial(finish_kernel, bins),
        out_shape=tuple(outputs.values()),
        in_specs=[ANY, VMEM, VMEM],
        out_specs=(ANY, VMEM, VMEM),
        scratch_shapes=[dma((8,))],
        compiler_params=pltpu.CompilerParams(vmem_limit_bytes=60 * 2**20),
        name="finish",
    )(prediction, grad_kernel, grad_bins)
    return prediction.transpose(2, 0, 1), grad_kernel.reshape(kernel.shape), grad_bins


def solution(mesh):
    in_specs = (P("row", None), P(), P("row", "col", None))
    out_specs = (P("row", "col", None), P(), P("row", None))
    return jax.shard_map(
        functools.partial(on_device, mesh.shape["row"], mesh.shape["col"]),
        mesh=mesh,
        in_specs=in_specs,
        out_specs=out_specs,
        check_vma=False,
    )
```

```python
import functools
import types

import jax
import jax.numpy as jnp
from jax import lax
from jax.experimental import pallas as pl
from jax.experimental.pallas import tpu as pltpu
from jax.sharding import PartitionSpec as P

STEP = 8
MESH = pl.DeviceIdType.MESH
VMEM = pl.BlockSpec(memory_space=pltpu.VMEM)
ANY = pl.BlockSpec(memory_space=pl.ANY)


def signal(barrier, row, col):
    pl.semaphore_signal(barrier, inc=1, device_id=(row, col), device_id_type=MESH)


def remote(src, dst, send, recv, row, col):
    return pltpu.make_async_remote_copy(
        src_ref=src,
        dst_ref=dst,
        send_sem=send,
        recv_sem=recv,
        device_id=(row, col),
        device_id_type=MESH,
    )


def tile_kernel(n_row, n_col, chunk, piece, refs):
    emb_hbm, kernel_hbm, cot_hbm = refs.emb_hbm, refs.kernel_hbm, refs.cot_hbm
    wide_ref, weight_ref, cot_ref, pred_ref = refs.wide, refs.weight, refs.cot, refs.pred
    act_ref, turned_ref, grad_ref, product_ref = refs.act, refs.turned, refs.grad, refs.product
    col_ref, partial, total, every = refs.col, refs.partial, refs.total, refs.every
    columns, channels, rows = cot_ref.shape
    half = columns // 2
    blocks = half // STEP
    span = rows + 2 * STEP
    depth = half + 2 * STEP
    lanes = 2 * channels
    bins = n_row * rows
    size = chunk + span
    ratio = rows // columns
    row, col = lax.axis_index("row"), lax.axis_index("col")
    row0, col0 = row * rows, col * columns
    owner = col // ratio
    row_peers = [lax.rem(row + d, n_row) for d in range(1, n_row)]
    col_peers = [lax.rem(col + d, n_col) for d in range(1, n_col)]

    def local(source, target, sem):
        return pltpu.make_async_copy(source, target, sem)

    def cot_copy(n, h):
        at = pl.ds(h * half + n * STEP, STEP)
        return local(cot_hbm.at[at], cot_ref.at[at], refs.cot_sem.at[n, h])

    def pred_copy(n, h):
        at = pl.ds(h * half + n * STEP, STEP)
        return local(pred_ref.at[at], refs.pred_hbm.at[at], refs.pred_sem.at[n, h])

    def rows_at(index, count):
        return pl.ds(pl.multiple_of(index * count, STEP), count)

    def start(copies):
        for copy in copies:
            copy.start()

    def wait(copies):
        for copy in copies:
            copy.wait()

    barrier = pltpu.get_barrier_semaphore()
    for peer in row_peers:
        signal(barrier, peer, col)
    for peer in col_peers:
        signal(barrier, row, peer)
    inputs = [
        local(emb_hbm, refs.emb, refs.in_sem.at[0]),
        local(kernel_hbm, refs.kernel, refs.in_sem.at[1]),
    ]
    start(inputs)
    start([cot_copy(n, h) for n in range(blocks) for h in range(2)])

    grad_ref[...] = jnp.zeros_like(grad_ref)
    product_ref[...] = jnp.zeros_like(product_ref)
    zeros = jnp.zeros((STEP, lanes), jnp.float32)
    wide_ref[:STEP] = zeros
    wide_ref[STEP + bins :] = zeros
    if n_col * piece > size:
        partial[size:] = jnp.zeros((n_col * piece - size, lanes), jnp.float32)

    wait(inputs)
    pl.semaphore_wait(barrier, n_row + n_col - 2)
    gather = [
        remote(refs.emb, refs.held.at[d], refs.send_g.at[d], refs.recv_g.at[d], peer, col)
        for d, peer in enumerate(row_peers)
    ]
    start(gather)

    none = jnp.zeros((channels, channels), jnp.float32)
    for a in range(3):
        for b in range(3):
            w = refs.kernel[a, b].astype(jnp.float32)
            both = jnp.concatenate(
                [jnp.concatenate([w, none], axis=1), jnp.concatenate([none, w], axis=1)], axis=0
            )
            weight_ref[b * lanes : (b + 1) * lanes, a * lanes : (a + 1) * lanes] = both.astype(
                jnp.bfloat16
            )

    def spread(n, carry):
        wait([cot_copy(n, h) for h in range(2)])
        cot = []
        for k in range(STEP):
            at = n * STEP + k
            stack = jnp.concatenate([cot_ref[at], cot_ref[half + at]], axis=0)
            cot.append(stack.astype(jnp.float32).T)
        cot = jnp.stack(cot)
        zero = jnp.zeros((STEP, STEP, lanes), jnp.float32)
        shifted = [
            jnp.concatenate([zero] * a + [cot] + [zero] * (2 - a), axis=1).astype(jnp.bfloat16)
            for a in range(3)
        ]
        y = jnp.concatenate(shifted, axis=2).reshape(STEP * span, 3 * lanes)
        turned_ref[n] = y
        back = lax.dot_general(
            y, weight_ref[...], (((1,), (1,)), ((), ())), preferred_element_type=jnp.float32
        ).reshape(STEP, span, 3 * lanes)
        for b in range(3):
            grad_ref[n + b] += back[:, :, b * lanes : (b + 1) * lanes]
        return carry

    lax.fori_loop(0, blocks, spread, 0)

    wide_ref[pl.ds(pl.multiple_of(STEP + row0, STEP), rows)] = refs.emb[...].astype(jnp.float32)
    for d, copy in enumerate(gather):
        copy.wait()
        peer = lax.rem(row + n_row - 1 - d, n_row)
        at = pl.ds(pl.multiple_of(STEP + peer * rows, STEP), rows)
        wide_ref[at] = refs.held[d].astype(jnp.float32)

    def first(shape):
        return lax.broadcasted_iota(jnp.int32, shape, len(shape) - 1) < channels

    def swap(x):
        return pltpu.roll(x, channels, 1)

    low = wide_ref[pl.ds(pl.multiple_of(col0, STEP), depth)]
    high = wide_ref[pl.ds(pl.multiple_of(col0 + half, STEP), depth)]
    in_first = first((depth, lanes))
    refs.u_col[...] = jnp.where(in_first, low, swap(high))
    refs.v_col[...] = jnp.where(in_first, swap(low), high)
    side = wide_ref[pl.ds(pl.multiple_of(row0, STEP), span)]
    in_first_row = first((span, lanes))
    u_row = jnp.where(in_first_row, side, swap(side))
    v_row = jnp.where(in_first_row, swap(side), side)
    row_pos = row0 - STEP + lax.broadcasted_iota(jnp.int32, (span, lanes), 0)
    row_in = jnp.where((row_pos >= 0) & (row_pos < bins), 1.0, 0.0)

    def activate(m, carry):
        u_total, v_total = carry
        at = pl.ds(pl.multiple_of(m * STEP, STEP), STEP)
        shape = (STEP, 1, lanes)
        pos = col0 - STEP + m * STEP + lax.broadcasted_iota(jnp.int32, shape, 0)
        pos = pos + jnp.where(first(shape), 0, half)
        col_in = jnp.where((pos >= 0) & (pos < bins), 1.0, 0.0)
        u_col = refs.u_col[at][:, None, :]
        pairs = u_col * u_row[None] + refs.v_col[at][:, None, :] + v_row[None]
        s = 0.5 * jnp.tanh(0.5 * pairs) + 0.5
        s = s * (col_in * row_in[None])
        act = pairs * s
        act_ref[m] = act.reshape(STEP * span, lanes).astype(jnp.bfloat16)
        grad = grad_ref[m] * (s + act * (1.0 - s))
        refs.u_sum[at] = jnp.sum(grad * u_row[None], axis=1)
        refs.v_sum[at] = jnp.sum(grad, axis=1)
        u_total = u_total + jnp.sum(grad * u_col, axis=0)
        return u_total, v_total + jnp.sum(grad, axis=0)

    nothing = jnp.zeros((span, lanes), jnp.float32)
    u_total, v_total = lax.fori_loop(0, blocks + 2, activate, (nothing, nothing))

    row_part = jnp.where(in_first_row, u_total + swap(u_total), v_total + swap(v_total))
    partial[chunk:size] = row_part
    u_sum, v_sum = refs.u_sum[...], refs.v_sum[...]
    col_ref[:depth] = jnp.where(in_first, u_sum, swap(v_sum))
    col_ref[depth:] = jnp.zeros((half, lanes), jnp.float32)
    col_ref[half:] += jnp.where(in_first, swap(u_sum), v_sum)

    away = lax.rem(owner + n_row - row, n_row) - 1

    def owned_copy(d, target):
        return remote(
            col_ref, refs.from_owned.at[d], refs.send_e.at[0], refs.recv_e.at[d], target, col
        )

    @pl.when(row != owner)
    def _():
        owned_copy(away, owner).start()

    def lay(n):
        return jnp.concatenate([act_ref[n + b] for b in range(3)], axis=1)

    def multiply(n, carry):
        product_ref[...] += lax.dot_general(
            lay(n), turned_ref[n], (((0,), (0,)), ((), ())), preferred_element_type=jnp.float32
        )
        return carry

    lax.fori_loop(0, blocks, multiply, 0)
    for a in range(3):
        for b in range(3):
            block = product_ref[b * lanes : (b + 1) * lanes, a * lanes : (a + 1) * lanes]
            tap = (3 * a + b) * channels
            refs.flat[tap : tap + channels] = (
                block[:channels, :channels] + block[channels:, channels:]
            )
    taps = 9 * channels // 2
    refs.packed[:taps] = jnp.concatenate([refs.flat[:taps], refs.flat[taps:]], axis=1)
    if n_row * chunk > taps:
        refs.packed[taps:] = jnp.zeros((n_row * chunk - taps, lanes), jnp.float32)
    to_row = [
        remote(
            refs.packed.at[rows_at(peer, chunk)],
            refs.from_row.at[d],
            refs.send_a.at[d],
            refs.recv_a.at[d],
            peer,
            col,
        )
        for d, peer in enumerate(row_peers)
    ]
    start(to_row)

    def predict(n, carry):
        out = jnp.dot(lay(n), weight_ref[...], preferred_element_type=jnp.float32)
        out = out.reshape(STEP, span, 3 * lanes)
        out = (
            out[:, :rows, :lanes]
            + out[:, STEP : STEP + rows, lanes : 2 * lanes]
            + out[:, 2 * STEP :, 2 * lanes :]
        )
        for k in range(STEP):
            at = n * STEP + k
            turned = out[k].T
            pred_ref[at] = turned[:channels]
            pred_ref[half + at] = turned[channels:]
        start([pred_copy(n, h) for h in range(2)])
        return carry

    bounds = [blocks * part // 4 for part in (0, 1, 2, 4)]
    lax.fori_loop(bounds[0], bounds[1], predict, 0)

    @pl.when(row == owner)
    def _():
        mine = col_ref[...]
        for d in range(n_row - 1):
            owned_copy(d, row_peers[0]).wait_recv()
            mine = mine + refs.from_owned[d]
        begin = chunk + lax.rem(col, ratio) * columns
        partial[pl.ds(pl.multiple_of(begin, STEP), columns + 2 * STEP)] += mine

    @pl.when(row != owner)
    def _():
        owned_copy(away, owner).wait_send()

    wait(to_row)
    mine = refs.packed[rows_at(row, chunk)]
    for d in range(n_row - 1):
        mine = mine + refs.from_row[d]
    partial[:chunk] = mine

    to_col = [
        remote(
            partial.at[rows_at(peer, piece)],
            refs.from_col.at[d],
            refs.send_b.at[d],
            refs.recv_b.at[d],
            row,
            peer,
        )
        for d, peer in enumerate(col_peers)
    ]
    start(to_col)
    lax.fori_loop(bounds[1], bounds[2], predict, 0)
    wait(to_col)
    here = rows_at(col, piece)
    mine = partial[here]
    for d in range(n_col - 1):
        mine = mine + refs.from_col[d]
    total[here] = mine

    back_col = [
        remote(total.at[here], total.at[here], refs.send_c.at[d], refs.recv_c.at[d], row, peer)
        for d, peer in enumerate(col_peers)
    ]
    start(back_col)
    lax.fori_loop(bounds[2], bounds[3], predict, 0)
    wait(back_col)

    below, above = lax.rem(row + n_row - 1, n_row), lax.rem(row + 1, n_row)
    here = rows_at(row, chunk)
    last = [
        remote(
            total.at[pl.ds(begin, STEP)],
            refs.border.at[d],
            refs.send_f.at[d],
            refs.recv_f.at[d],
            peer,
            col,
        )
        for d, (peer, begin) in enumerate([(below, chunk), (above, size - STEP)])
    ] + [
        remote(
            total.at[pl.ds(0, chunk)], every.at[here], refs.send_d.at[d], refs.recv_d.at[d], peer, col
        )
        for d, peer in enumerate(row_peers)
    ]
    start(last)
    every[here] = total[:chunk]
    refs.bins_out[...] = total[chunk + STEP : size - STEP]
    wait(last)
    refs.bins_out[rows - STEP :] += refs.border[0]
    refs.bins_out[:STEP] += refs.border[1]
    refs.taps_out[:taps] = every[:taps, :channels]
    refs.taps_out[taps:] = every[:taps, channels:]
    wait([pred_copy(n, h) for n in range(blocks) for h in range(2)])


def finish_kernel(bins, pred_in, taps_in, bins_in, pred_out, taps_out, bins_out, held, sem):
    parts = sem.shape[1]
    count = pred_in.shape[0] // parts
    copies = []
    for part in range(parts):
        at = pl.ds(part * count, count)
        copy = pltpu.make_async_copy(pred_in.at[at], held.at[at], sem.at[0, part])
        copy.start()
        copies.append(copy)
    taps_out[...] = taps_in[...] / bins
    bins_out[...] = bins_in[...] * float(bins) ** (-0.5)
    for part in range(parts):
        copies[part].wait()
        at = pl.ds(part * count, count)
        copy = pltpu.make_async_copy(held.at[at], pred_out.at[at], sem.at[1, part])
        copy.start()
        copies.append(copy)
    for copy in copies[parts:]:
        copy.wait()


def round_up(value, step):
    return -(-value // step) * step


def on_device(n_row, n_col, embedding, kernel, cotangent):
    rows, columns, channels = cotangent.shape
    lanes = 2 * channels
    bins = n_row * rows
    half = columns // 2
    blocks = half // STEP
    span = rows + 2 * STEP
    depth = half + 2 * STEP
    taps = 9 * channels
    chunk = round_up(-(-taps // (2 * n_row)), STEP)
    piece = round_up(-(-(chunk + span) // n_col), STEP)
    f32, bf16 = jnp.float32, jnp.bfloat16
    dma = pltpu.SemaphoreType.DMA
    outputs = {
        "pred_hbm": jax.ShapeDtypeStruct((columns, channels, rows), f32),
        "taps_out": jax.ShapeDtypeStruct((taps, channels), f32),
        "bins_out": jax.ShapeDtypeStruct((rows, lanes), f32),
    }
    scratch = {
        "emb": pltpu.VMEM((rows, lanes), bf16),
        "kernel": pltpu.VMEM(kernel.shape, bf16),
        "cot": pltpu.VMEM((columns, channels, rows), bf16),
        "pred": pltpu.VMEM((columns, channels, rows), f32),
        "held": pltpu.VMEM((n_row - 1, rows, lanes), bf16),
        "wide": pltpu.VMEM((bins + 2 * STEP, lanes), f32),
        "weight": pltpu.VMEM((3 * lanes, 3 * lanes), bf16),
        "u_col": pltpu.VMEM((depth, lanes), f32),
        "v_col": pltpu.VMEM((depth, lanes), f32),
        "act": pltpu.VMEM((blocks + 2, STEP * span, lanes), bf16),
        "turned": pltpu.VMEM((blocks, STEP * span, 3 * lanes), bf16),
        "grad": pltpu.VMEM((blocks + 2, STEP, span, lanes), f32),
        "product": pltpu.VMEM((3 * lanes, 3 * lanes), f32),
        "u_sum": pltpu.VMEM((depth, lanes), f32),
        "v_sum": pltpu.VMEM((depth, lanes), f32),
        "flat": pltpu.VMEM((taps, channels), f32),
        "packed": pltpu.VMEM((n_row * chunk, lanes), f32),
        "col": pltpu.VMEM((columns + 2 * STEP, lanes), f32),
        "from_row": pltpu.VMEM((n_row - 1, chunk, lanes), f32),
        "from_owned": pltpu.VMEM((n_row - 1, columns + 2 * STEP, lanes), f32),
        "partial": pltpu.VMEM((n_col * piece, lanes), f32),
        "from_col": pltpu.VMEM((n_col - 1, piece, lanes), f32),
        "total": pltpu.VMEM((n_col * piece, lanes), f32),
        "every": pltpu.VMEM((n_row * chunk, lanes), f32),
        "border": pltpu.VMEM((2, STEP, lanes), f32),
        "in_sem": dma((2,)),
        "cot_sem": dma((blocks, 2)),
        "pred_sem": dma((blocks, 2)),
        "send_g": dma((n_row - 1,)),
        "recv_g": dma((n_row - 1,)),
        "send_a": dma((n_row - 1,)),
        "recv_a": dma((n_row - 1,)),
        "send_b": dma((n_col - 1,)),
        "recv_b": dma((n_col - 1,)),
        "send_c": dma((n_col - 1,)),
        "recv_c": dma((n_col - 1,)),
        "send_d": dma((n_row - 1,)),
        "recv_d": dma((n_row - 1,)),
        "send_e": dma((1,)),
        "recv_e": dma((n_row - 1,)),
        "send_f": dma((2,)),
        "recv_f": dma((2,)),
    }
    names = ["emb_hbm", "kernel_hbm", "cot_hbm", *outputs, *scratch]

    def tile(*refs):
        tile_kernel(n_row, n_col, chunk, piece, types.SimpleNamespace(**dict(zip(names, refs))))

    prediction, grad_kernel, grad_bins = pl.pallas_call(
        tile,
        out_shape=tuple(outputs.values()),
        in_specs=[ANY, ANY, ANY],
        out_specs=(ANY, VMEM, VMEM),
        scratch_shapes=list(scratch.values()),
        compiler_params=pltpu.CompilerParams(
            collective_id=0, has_side_effects=True, vmem_limit_bytes=60 * 2**20
        ),
        name="tile_gradients",
    )(embedding, kernel, cotangent.transpose(1, 2, 0))

    prediction, grad_kernel, grad_bins = pl.pallas_call(
        functools.partial(finish_kernel, bins),
        out_shape=tuple(outputs.values()),
        in_specs=[ANY, VMEM, VMEM],
        out_specs=(ANY, VMEM, VMEM),
        scratch_shapes=[pltpu.VMEM((columns, channels, rows), f32), dma((2, 8))],
        compiler_params=pltpu.CompilerParams(vmem_limit_bytes=60 * 2**20),
        name="finish",
    )(prediction, grad_kernel, grad_bins)
    return prediction.transpose(2, 0, 1), grad_kernel.reshape(kernel.shape), grad_bins


def solution(mesh):
    in_specs = (P("row", None), P(), P("row", "col", None))
    out_specs = (P("row", "col", None), P(), P("row", None))
    return jax.shard_map(
        functools.partial(on_device, mesh.shape["row"], mesh.shape["col"]),
        mesh=mesh,
        in_specs=in_specs,
        out_specs=out_specs,
        check_vma=False,
    )
```

```python
import functools
import types

import jax
import jax.numpy as jnp
from jax import lax
from jax.experimental import pallas as pl
from jax.experimental.pallas import tpu as pltpu
from jax.sharding import PartitionSpec as P

STEP = 8
MESH = pl.DeviceIdType.MESH
VMEM = pl.BlockSpec(memory_space=pltpu.VMEM)
HBM = pl.BlockSpec(memory_space=pltpu.HBM)


def signal(barrier, row, col):
    pl.semaphore_signal(barrier, inc=1, device_id=(row, col), device_id_type=MESH)


def remote(src, dst, send, recv, row, col):
    return pltpu.make_async_remote_copy(
        src_ref=src,
        dst_ref=dst,
        send_sem=send,
        recv_sem=recv,
        device_id=(row, col),
        device_id_type=MESH,
    )


def tile_kernel(n_row, n_col, chunk, piece, refs):
    emb_hbm, kernel_hbm, cot_hbm = refs.emb_hbm, refs.kernel_hbm, refs.cot_hbm
    wide_ref, weight_ref, cot_ref, pred_ref = refs.wide, refs.weight, refs.cot, refs.pred
    act_ref, turned_ref, grad_ref, product_ref = refs.act, refs.turned, refs.grad, refs.product
    col_ref, partial, total, every = refs.col, refs.partial, refs.total, refs.every
    columns, channels, rows = cot_ref.shape
    half = columns // 2
    blocks = half // STEP
    span = rows + 2 * STEP
    depth = half + 2 * STEP
    lanes = 2 * channels
    bins = n_row * rows
    size = chunk + span
    ratio = rows // columns
    row, col = lax.axis_index("row"), lax.axis_index("col")
    row0, col0 = row * rows, col * columns
    owner = col // ratio
    row_peers = [lax.rem(row + d, n_row) for d in range(1, n_row)]
    col_peers = [lax.rem(col + d, n_col) for d in range(1, n_col)]

    def local(source, target, sem):
        return pltpu.make_async_copy(source, target, sem)

    def cot_copy(n, h):
        at = pl.ds(h * half + n * STEP, STEP)
        return local(cot_hbm.at[at], cot_ref.at[at], refs.cot_sem.at[n, h])

    def rows_at(index, count):
        return pl.ds(pl.multiple_of(index * count, STEP), count)

    def start(copies):
        for copy in copies:
            copy.start()

    def wait(copies):
        for copy in copies:
            copy.wait()

    barrier = pltpu.get_barrier_semaphore()
    for peer in row_peers:
        signal(barrier, peer, col)
    for peer in col_peers:
        signal(barrier, row, peer)
    inputs = [
        local(emb_hbm, refs.emb, refs.in_sem.at[0]),
        local(kernel_hbm, refs.kernel, refs.in_sem.at[1]),
    ]
    start(inputs)
    start([cot_copy(n, h) for n in range(blocks) for h in range(2)])

    grad_ref[...] = jnp.zeros_like(grad_ref)
    product_ref[...] = jnp.zeros_like(product_ref)
    zeros = jnp.zeros((STEP, lanes), jnp.float32)
    wide_ref[:STEP] = zeros
    wide_ref[STEP + bins :] = zeros
    if n_col * piece > size:
        partial[size:] = jnp.zeros((n_col * piece - size, lanes), jnp.float32)

    wait(inputs)
    pl.semaphore_wait(barrier, n_row + n_col - 2)
    gather = [
        remote(refs.emb, refs.held.at[d], refs.send_g.at[d], refs.recv_g.at[d], peer, col)
        for d, peer in enumerate(row_peers)
    ]
    start(gather)

    none = jnp.zeros((channels, channels), jnp.float32)
    for a in range(3):
        for b in range(3):
            w = refs.kernel[a, b].astype(jnp.float32)
            both = jnp.concatenate(
                [jnp.concatenate([w, none], axis=1), jnp.concatenate([none, w], axis=1)], axis=0
            )
            weight_ref[b * lanes : (b + 1) * lanes, a * lanes : (a + 1) * lanes] = both.astype(
                jnp.bfloat16
            )

    def spread(n, carry):
        wait([cot_copy(n, h) for h in range(2)])
        cot = []
        for k in range(STEP):
            at = n * STEP + k
            stack = jnp.concatenate([cot_ref[at], cot_ref[half + at]], axis=0)
            cot.append(stack.astype(jnp.float32).T)
        cot = jnp.stack(cot)
        zero = jnp.zeros((STEP, STEP, lanes), jnp.float32)
        shifted = [
            jnp.concatenate([zero] * a + [cot] + [zero] * (2 - a), axis=1).astype(jnp.bfloat16)
            for a in range(3)
        ]
        y = jnp.concatenate(shifted, axis=2).reshape(STEP * span, 3 * lanes)
        turned_ref[n] = y
        back = lax.dot_general(
            y, weight_ref[...], (((1,), (1,)), ((), ())), preferred_element_type=jnp.float32
        ).reshape(STEP, span, 3 * lanes)
        for b in range(3):
            grad_ref[n + b] += back[:, :, b * lanes : (b + 1) * lanes]
        return carry

    lax.fori_loop(0, blocks, spread, 0)

    wide_ref[pl.ds(pl.multiple_of(STEP + row0, STEP), rows)] = refs.emb[...].astype(jnp.float32)
    for d, copy in enumerate(gather):
        copy.wait()
        peer = lax.rem(row + n_row - 1 - d, n_row)
        at = pl.ds(pl.multiple_of(STEP + peer * rows, STEP), rows)
        wide_ref[at] = refs.held[d].astype(jnp.float32)

    def first(shape):
        return lax.broadcasted_iota(jnp.int32, shape, len(shape) - 1) < channels

    def swap(x):
        return pltpu.roll(x, channels, 1)

    low = wide_ref[pl.ds(pl.multiple_of(col0, STEP), depth)]
    high = wide_ref[pl.ds(pl.multiple_of(col0 + half, STEP), depth)]
    in_first = first((depth, lanes))
    refs.u_col[...] = jnp.where(in_first, low, swap(high))
    refs.v_col[...] = jnp.where(in_first, swap(low), high)
    side = wide_ref[pl.ds(pl.multiple_of(row0, STEP), span)]
    in_first_row = first((span, lanes))
    u_row = jnp.where(in_first_row, side, swap(side))
    v_row = jnp.where(in_first_row, swap(side), side)
    row_pos = row0 - STEP + lax.broadcasted_iota(jnp.int32, (span, lanes), 0)
    row_in = jnp.where((row_pos >= 0) & (row_pos < bins), 1.0, 0.0)

    def activate(m, carry):
        u_total, v_total = carry
        at = pl.ds(pl.multiple_of(m * STEP, STEP), STEP)
        shape = (STEP, 1, lanes)
        pos = col0 - STEP + m * STEP + lax.broadcasted_iota(jnp.int32, shape, 0)
        pos = pos + jnp.where(first(shape), 0, half)
        col_in = jnp.where((pos >= 0) & (pos < bins), 1.0, 0.0)
        u_col = refs.u_col[at][:, None, :]
        pairs = u_col * u_row[None] + refs.v_col[at][:, None, :] + v_row[None]
        s = 0.5 * jnp.tanh(0.5 * pairs) + 0.5
        s = s * (col_in * row_in[None])
        act = pairs * s
        act_ref[m] = act.reshape(STEP * span, lanes).astype(jnp.bfloat16)
        grad = grad_ref[m] * (s + act * (1.0 - s))
        refs.u_sum[at] = jnp.sum(grad * u_row[None], axis=1)
        refs.v_sum[at] = jnp.sum(grad, axis=1)
        u_total = u_total + jnp.sum(grad * u_col, axis=0)
        return u_total, v_total + jnp.sum(grad, axis=0)

    nothing = jnp.zeros((span, lanes), jnp.float32)
    u_total, v_total = lax.fori_loop(0, blocks + 2, activate, (nothing, nothing))

    row_part = jnp.where(in_first_row, u_total + swap(u_total), v_total + swap(v_total))
    partial[chunk:size] = row_part
    u_sum, v_sum = refs.u_sum[...], refs.v_sum[...]
    col_ref[:depth] = jnp.where(in_first, u_sum, swap(v_sum))
    col_ref[depth:] = jnp.zeros((half, lanes), jnp.float32)
    col_ref[half:] += jnp.where(in_first, swap(u_sum), v_sum)

    away = lax.rem(owner + n_row - row, n_row) - 1

    def owned_copy(d, target):
        return remote(
            col_ref, refs.from_owned.at[d], refs.send_e.at[0], refs.recv_e.at[d], target, col
        )

    @pl.when(row != owner)
    def _():
        owned_copy(away, owner).start()

    def lay(n):
        return jnp.concatenate([act_ref[n + b] for b in range(3)], axis=1)

    def multiply(n, carry):
        product_ref[...] += lax.dot_general(
            lay(n), turned_ref[n], (((0,), (0,)), ((), ())), preferred_element_type=jnp.float32
        )
        return carry

    lax.fori_loop(0, blocks, multiply, 0)
    for a in range(3):
        for b in range(3):
            block = product_ref[b * lanes : (b + 1) * lanes, a * lanes : (a + 1) * lanes]
            tap = (3 * a + b) * channels
            refs.flat[tap : tap + channels] = (
                block[:channels, :channels] + block[channels:, channels:]
            )
    taps = 9 * channels // 2
    refs.packed[:taps] = jnp.concatenate([refs.flat[:taps], refs.flat[taps:]], axis=1)
    if n_row * chunk > taps:
        refs.packed[taps:] = jnp.zeros((n_row * chunk - taps, lanes), jnp.float32)
    to_row = [
        remote(
            refs.packed.at[rows_at(peer, chunk)],
            refs.from_row.at[d],
            refs.send_a.at[d],
            refs.recv_a.at[d],
            peer,
            col,
        )
        for d, peer in enumerate(row_peers)
    ]
    start(to_row)

    def predict(n, carry):
        out = jnp.dot(lay(n), weight_ref[...], preferred_element_type=jnp.float32)
        out = out.reshape(STEP, span, 3 * lanes)
        out = (
            out[:, :rows, :lanes]
            + out[:, STEP : STEP + rows, lanes : 2 * lanes]
            + out[:, 2 * STEP :, 2 * lanes :]
        )
        for k in range(STEP):
            at = n * STEP + k
            turned = out[k].T
            pred_ref[at] = turned[:channels]
            pred_ref[half + at] = turned[channels:]
        return carry

    bounds = [blocks * part // 4 for part in (0, 1, 2, 4)]
    lax.fori_loop(bounds[0], bounds[1], predict, 0)

    @pl.when(row == owner)
    def _():
        mine = col_ref[...]
        for d in range(n_row - 1):
            owned_copy(d, row_peers[0]).wait_recv()
            mine = mine + refs.from_owned[d]
        begin = chunk + lax.rem(col, ratio) * columns
        partial[pl.ds(pl.multiple_of(begin, STEP), columns + 2 * STEP)] += mine

    @pl.when(row != owner)
    def _():
        owned_copy(away, owner).wait_send()

    wait(to_row)
    mine = refs.packed[rows_at(row, chunk)]
    for d in range(n_row - 1):
        mine = mine + refs.from_row[d]
    partial[:chunk] = mine

    to_col = [
        remote(
            partial.at[rows_at(peer, piece)],
            refs.from_col.at[d],
            refs.send_b.at[d],
            refs.recv_b.at[d],
            row,
            peer,
        )
        for d, peer in enumerate(col_peers)
    ]
    start(to_col)
    lax.fori_loop(bounds[1], bounds[2], predict, 0)
    wait(to_col)
    here = rows_at(col, piece)
    mine = partial[here]
    for d in range(n_col - 1):
        mine = mine + refs.from_col[d]
    total[here] = mine

    back_col = [
        remote(total.at[here], total.at[here], refs.send_c.at[d], refs.recv_c.at[d], row, peer)
        for d, peer in enumerate(col_peers)
    ]
    start(back_col)
    lax.fori_loop(bounds[2], bounds[3], predict, 0)
    wait(back_col)

    below, above = lax.rem(row + n_row - 1, n_row), lax.rem(row + 1, n_row)
    here = rows_at(row, chunk)
    last = [
        remote(
            total.at[pl.ds(begin, STEP)],
            refs.border.at[d],
            refs.send_f.at[d],
            refs.recv_f.at[d],
            peer,
            col,
        )
        for d, (peer, begin) in enumerate([(below, chunk), (above, size - STEP)])
    ] + [
        remote(
            total.at[pl.ds(0, chunk)], every.at[here], refs.send_d.at[d], refs.recv_d.at[d], peer, col
        )
        for d, peer in enumerate(row_peers)
    ]
    start(last)
    every[here] = total[:chunk]
    refs.bins_out[...] = total[chunk + STEP : size - STEP]
    wait(last)
    refs.bins_out[rows - STEP :] += refs.border[0]
    refs.bins_out[:STEP] += refs.border[1]
    refs.taps_out[:taps] = every[:taps, :channels]
    refs.taps_out[taps:] = every[:taps, channels:]


def finish_kernel(
    bins, pred_in, taps_in, bins_in, pred_out, taps_out, bins_out, taps_ref, bins_ref, sem
):
    copies = [
        pltpu.make_async_copy(pred_in, pred_out, sem.at[0]),
        pltpu.make_async_copy(taps_ref, taps_out, sem.at[1]),
        pltpu.make_async_copy(bins_ref, bins_out, sem.at[2]),
    ]
    copies[0].start()
    taps_ref[...] = taps_in[...] / bins
    copies[1].start()
    bins_ref[...] = bins_in[...] * float(bins) ** (-0.5)
    copies[2].start()
    for copy in copies:
        copy.wait()


def in_hbm(x):
    return pltpu.with_memory_space_constraint(x, pltpu.HBM)


def round_up(value, step):
    return -(-value // step) * step


def on_device(n_row, n_col, embedding, kernel, cotangent):
    rows, columns, channels = cotangent.shape
    lanes = 2 * channels
    bins = n_row * rows
    half = columns // 2
    blocks = half // STEP
    span = rows + 2 * STEP
    depth = half + 2 * STEP
    taps = 9 * channels
    chunk = round_up(-(-taps // (2 * n_row)), STEP)
    piece = round_up(-(-(chunk + span) // n_col), STEP)
    f32, bf16 = jnp.float32, jnp.bfloat16
    dma = pltpu.SemaphoreType.DMA
    outputs = {
        "pred": jax.ShapeDtypeStruct((columns, channels, rows), f32),
        "taps_out": jax.ShapeDtypeStruct((taps, channels), f32),
        "bins_out": jax.ShapeDtypeStruct((rows, lanes), f32),
    }
    scratch = {
        "emb": pltpu.VMEM((rows, lanes), bf16),
        "kernel": pltpu.VMEM(kernel.shape, bf16),
        "cot": pltpu.VMEM((columns, channels, rows), bf16),
        "held": pltpu.VMEM((n_row - 1, rows, lanes), bf16),
        "wide": pltpu.VMEM((bins + 2 * STEP, lanes), f32),
        "weight": pltpu.VMEM((3 * lanes, 3 * lanes), bf16),
        "u_col": pltpu.VMEM((depth, lanes), f32),
        "v_col": pltpu.VMEM((depth, lanes), f32),
        "act": pltpu.VMEM((blocks + 2, STEP * span, lanes), bf16),
        "turned": pltpu.VMEM((blocks, STEP * span, 3 * lanes), bf16),
        "grad": pltpu.VMEM((blocks + 2, STEP, span, lanes), f32),
        "product": pltpu.VMEM((3 * lanes, 3 * lanes), f32),
        "u_sum": pltpu.VMEM((depth, lanes), f32),
        "v_sum": pltpu.VMEM((depth, lanes), f32),
        "flat": pltpu.VMEM((taps, channels), f32),
        "packed": pltpu.VMEM((n_row * chunk, lanes), f32),
        "col": pltpu.VMEM((columns + 2 * STEP, lanes), f32),
        "from_row": pltpu.VMEM((n_row - 1, chunk, lanes), f32),
        "from_owned": pltpu.VMEM((n_row - 1, columns + 2 * STEP, lanes), f32),
        "partial": pltpu.VMEM((n_col * piece, lanes), f32),
        "from_col": pltpu.VMEM((n_col - 1, piece, lanes), f32),
        "total": pltpu.VMEM((n_col * piece, lanes), f32),
        "every": pltpu.VMEM((n_row * chunk, lanes), f32),
        "border": pltpu.VMEM((2, STEP, lanes), f32),
        "in_sem": dma((2,)),
        "cot_sem": dma((blocks, 2)),
        "send_g": dma((n_row - 1,)),
        "recv_g": dma((n_row - 1,)),
        "send_a": dma((n_row - 1,)),
        "recv_a": dma((n_row - 1,)),
        "send_b": dma((n_col - 1,)),
        "recv_b": dma((n_col - 1,)),
        "send_c": dma((n_col - 1,)),
        "recv_c": dma((n_col - 1,)),
        "send_d": dma((n_row - 1,)),
        "recv_d": dma((n_row - 1,)),
        "send_e": dma((1,)),
        "recv_e": dma((n_row - 1,)),
        "send_f": dma((2,)),
        "recv_f": dma((2,)),
    }
    names = ["emb_hbm", "kernel_hbm", "cot_hbm", *outputs, *scratch]

    def tile(*refs):
        tile_kernel(n_row, n_col, chunk, piece, types.SimpleNamespace(**dict(zip(names, refs))))

    prediction, grad_kernel, grad_bins = pl.pallas_call(
        tile,
        out_shape=tuple(outputs.values()),
        in_specs=[HBM, HBM, HBM],
        out_specs=(VMEM, VMEM, VMEM),
        scratch_shapes=list(scratch.values()),
        compiler_params=pltpu.CompilerParams(
            collective_id=0, has_side_effects=True, vmem_limit_bytes=32 * 2**20
        ),
        name="tile_gradients",
    )(*[in_hbm(x) for x in (embedding, kernel, cotangent.transpose(1, 2, 0))])

    prediction, grad_kernel, grad_bins = pl.pallas_call(
        functools.partial(finish_kernel, bins),
        out_shape=tuple(outputs.values()),
        in_specs=[VMEM, VMEM, VMEM],
        out_specs=(HBM, HBM, HBM),
        scratch_shapes=[
            pltpu.VMEM((taps, channels), f32),
            pltpu.VMEM((rows, lanes), f32),
            dma((3,)),
        ],
        compiler_params=pltpu.CompilerParams(vmem_limit_bytes=24 * 2**20),
        name="finish",
    )(prediction, grad_kernel, grad_bins)
    return prediction.transpose(2, 0, 1), grad_kernel.reshape(kernel.shape), grad_bins


def solution(mesh):
    in_specs = (P("row", None), P(), P("row", "col", None))
    out_specs = (P("row", "col", None), P(), P("row", None))
    return jax.shard_map(
        functools.partial(on_device, mesh.shape["row"], mesh.shape["col"]),
        mesh=mesh,
        in_specs=in_specs,
        out_specs=out_specs,
        check_vma=False,
    )
```

```python
import functools
import types

import jax
import jax.numpy as jnp
from jax import lax
from jax.experimental import pallas as pl
from jax.experimental.pallas import tpu as pltpu
from jax.sharding import PartitionSpec as P

STEP = 8
MESH = pl.DeviceIdType.MESH
VMEM = pl.BlockSpec(memory_space=pltpu.VMEM)
HBM = pl.BlockSpec(memory_space=pltpu.HBM)


def signal(barrier, row, col):
    pl.semaphore_signal(barrier, inc=1, device_id=(row, col), device_id_type=MESH)


def remote(src, dst, send, recv, row, col):
    return pltpu.make_async_remote_copy(
        src_ref=src,
        dst_ref=dst,
        send_sem=send,
        recv_sem=recv,
        device_id=(row, col),
        device_id_type=MESH,
    )


def tile_kernel(n_row, n_col, chunk, refs):
    emb_hbm, kernel_hbm, cot_hbm = refs.emb_hbm, refs.kernel_hbm, refs.cot_hbm
    wide_ref, weight_ref, cot_ref, pred_ref = refs.wide, refs.weight, refs.cot, refs.pred
    act_ref, turned_ref, grad_ref, product_ref = refs.act, refs.turned, refs.grad, refs.product
    col_ref, every = refs.col, refs.every
    bins_sum, taps_sum = refs.bins_sum, refs.taps_sum
    bins_total, taps_total = refs.bins_total, refs.taps_total
    columns, channels, rows = cot_ref.shape
    half = columns // 2
    blocks = half // STEP
    span = rows + 2 * STEP
    depth = half + 2 * STEP
    lanes = 2 * channels
    bins = n_row * rows
    ratio = rows // columns
    row, col = lax.axis_index("row"), lax.axis_index("col")
    row0, col0 = row * rows, col * columns
    owner = col // ratio
    row_peers = [lax.rem(row + d, n_row) for d in range(1, n_row)]
    col_peers = [lax.rem(col + d, n_col) for d in range(1, n_col)]

    def local(source, target, sem):
        return pltpu.make_async_copy(source, target, sem)

    def cot_copy(n, h):
        at = pl.ds(h * half + n * STEP, STEP)
        return local(cot_hbm.at[at], cot_ref.at[at], refs.cot_sem.at[n, h])

    def rows_at(index, count):
        return pl.ds(pl.multiple_of(index * count, STEP), count)

    def start(copies):
        for copy in copies:
            copy.start()

    def wait(copies):
        for copy in copies:
            copy.wait()

    barrier = pltpu.get_barrier_semaphore()
    for peer in row_peers:
        signal(barrier, peer, col)
    for peer in col_peers:
        signal(barrier, row, peer)
    inputs = [
        local(emb_hbm, refs.emb, refs.in_sem.at[0]),
        local(kernel_hbm, refs.kernel, refs.in_sem.at[1]),
    ]
    start(inputs)
    start([cot_copy(n, h) for n in range(blocks) for h in range(2)])

    grad_ref[...] = jnp.zeros_like(grad_ref)
    product_ref[...] = jnp.zeros_like(product_ref)
    zeros = jnp.zeros((STEP, lanes), jnp.float32)
    wide_ref[:STEP] = zeros
    wide_ref[STEP + bins :] = zeros
    for ref, used in [(bins_sum, span), (taps_sum, chunk)]:
        if ref.shape[0] > used:
            ref[used:] = jnp.zeros((ref.shape[0] - used, lanes), jnp.float32)

    wait(inputs)
    pl.semaphore_wait(barrier, n_row + n_col - 2)
    gather = [
        remote(refs.emb, refs.held.at[d], refs.send_g.at[d], refs.recv_g.at[d], peer, col)
        for d, peer in enumerate(row_peers)
    ]
    start(gather)

    none = jnp.zeros((channels, channels), jnp.float32)
    for a in range(3):
        for b in range(3):
            w = refs.kernel[a, b].astype(jnp.float32)
            both = jnp.concatenate(
                [jnp.concatenate([w, none], axis=1), jnp.concatenate([none, w], axis=1)], axis=0
            )
            weight_ref[b * lanes : (b + 1) * lanes, a * lanes : (a + 1) * lanes] = both.astype(
                jnp.bfloat16
            )

    def spread(n, carry):
        wait([cot_copy(n, h) for h in range(2)])
        cot = []
        for k in range(STEP):
            at = n * STEP + k
            stack = jnp.concatenate([cot_ref[at], cot_ref[half + at]], axis=0)
            cot.append(stack.astype(jnp.float32).T)
        cot = jnp.stack(cot)
        zero = jnp.zeros((STEP, STEP, lanes), jnp.float32)
        shifted = [
            jnp.concatenate([zero] * a + [cot] + [zero] * (2 - a), axis=1).astype(jnp.bfloat16)
            for a in range(3)
        ]
        y = jnp.concatenate(shifted, axis=2).reshape(STEP * span, 3 * lanes)
        turned_ref[n] = y
        back = lax.dot_general(
            y, weight_ref[...], (((1,), (1,)), ((), ())), preferred_element_type=jnp.float32
        ).reshape(STEP, span, 3 * lanes)
        for b in range(3):
            grad_ref[n + b] += back[:, :, b * lanes : (b + 1) * lanes]
        return carry

    lax.fori_loop(0, blocks, spread, 0)

    wide_ref[pl.ds(pl.multiple_of(STEP + row0, STEP), rows)] = refs.emb[...].astype(jnp.float32)
    for d, copy in enumerate(gather):
        copy.wait()
        peer = lax.rem(row + n_row - 1 - d, n_row)
        at = pl.ds(pl.multiple_of(STEP + peer * rows, STEP), rows)
        wide_ref[at] = refs.held[d].astype(jnp.float32)

    def first(shape):
        return lax.broadcasted_iota(jnp.int32, shape, len(shape) - 1) < channels

    def swap(x):
        return pltpu.roll(x, channels, 1)

    low = wide_ref[pl.ds(pl.multiple_of(col0, STEP), depth)]
    high = wide_ref[pl.ds(pl.multiple_of(col0 + half, STEP), depth)]
    in_first = first((depth, lanes))
    refs.u_col[...] = jnp.where(in_first, low, swap(high))
    refs.v_col[...] = jnp.where(in_first, swap(low), high)
    side = wide_ref[pl.ds(pl.multiple_of(row0, STEP), span)]
    in_first_row = first((span, lanes))
    u_row = jnp.where(in_first_row, side, swap(side))
    v_row = jnp.where(in_first_row, swap(side), side)
    row_pos = row0 - STEP + lax.broadcasted_iota(jnp.int32, (span, lanes), 0)
    row_in = jnp.where((row_pos >= 0) & (row_pos < bins), 1.0, 0.0)

    def activate(m, carry):
        u_total, v_total = carry
        at = pl.ds(pl.multiple_of(m * STEP, STEP), STEP)
        shape = (STEP, 1, lanes)
        pos = col0 - STEP + m * STEP + lax.broadcasted_iota(jnp.int32, shape, 0)
        pos = pos + jnp.where(first(shape), 0, half)
        col_in = jnp.where((pos >= 0) & (pos < bins), 1.0, 0.0)
        u_col = refs.u_col[at][:, None, :]
        pairs = u_col * u_row[None] + refs.v_col[at][:, None, :] + v_row[None]
        s = 0.5 * jnp.tanh(0.5 * pairs) + 0.5
        s = s * (col_in * row_in[None])
        act = pairs * s
        act_ref[m] = act.reshape(STEP * span, lanes).astype(jnp.bfloat16)
        grad = grad_ref[m] * (s + act * (1.0 - s))
        refs.u_sum[at] = jnp.sum(grad * u_row[None], axis=1)
        refs.v_sum[at] = jnp.sum(grad, axis=1)
        u_total = u_total + jnp.sum(grad * u_col, axis=0)
        return u_total, v_total + jnp.sum(grad, axis=0)

    nothing = jnp.zeros((span, lanes), jnp.float32)
    u_total, v_total = lax.fori_loop(0, blocks + 2, activate, (nothing, nothing))

    row_part = jnp.where(in_first_row, u_total + swap(u_total), v_total + swap(v_total))
    bins_sum[:span] = row_part
    u_sum, v_sum = refs.u_sum[...], refs.v_sum[...]
    col_ref[:depth] = jnp.where(in_first, u_sum, swap(v_sum))
    col_ref[depth:] = jnp.zeros((half, lanes), jnp.float32)
    col_ref[half:] += jnp.where(in_first, swap(u_sum), v_sum)

    away = lax.rem(owner + n_row - row, n_row) - 1

    def owned_copy(d, target):
        return remote(
            col_ref, refs.from_owned.at[d], refs.send_e.at[0], refs.recv_e.at[d], target, col
        )

    @pl.when(row != owner)
    def _():
        owned_copy(away, owner).start()

    def lay(n):
        return jnp.concatenate([act_ref[n + b] for b in range(3)], axis=1)

    def multiply(n, carry):
        product_ref[...] += lax.dot_general(
            lay(n), turned_ref[n], (((0,), (0,)), ((), ())), preferred_element_type=jnp.float32
        )
        return carry

    lax.fori_loop(0, blocks, multiply, 0)
    for a in range(3):
        for b in range(3):
            block = product_ref[b * lanes : (b + 1) * lanes, a * lanes : (a + 1) * lanes]
            tap = (3 * a + b) * channels
            refs.flat[tap : tap + channels] = (
                block[:channels, :channels] + block[channels:, channels:]
            )
    taps = 9 * channels // 2
    refs.packed[:taps] = jnp.concatenate([refs.flat[:taps], refs.flat[taps:]], axis=1)
    if n_row * chunk > taps:
        refs.packed[taps:] = jnp.zeros((n_row * chunk - taps, lanes), jnp.float32)
    to_row = [
        remote(
            refs.packed.at[rows_at(peer, chunk)],
            refs.from_row.at[d],
            refs.send_a.at[d],
            refs.recv_a.at[d],
            peer,
            col,
        )
        for d, peer in enumerate(row_peers)
    ]
    start(to_row)

    def predict(n, carry):
        out = jnp.dot(lay(n), weight_ref[...], preferred_element_type=jnp.float32)
        out = out.reshape(STEP, span, 3 * lanes)
        out = (
            out[:, :rows, :lanes]
            + out[:, STEP : STEP + rows, lanes : 2 * lanes]
            + out[:, 2 * STEP :, 2 * lanes :]
        )
        for k in range(STEP):
            at = n * STEP + k
            turned = out[k].T
            pred_ref[at] = turned[:channels]
            pred_ref[half + at] = turned[channels:]
        return carry

    def some(part):
        lax.fori_loop(blocks * part // 4, blocks * (part + 1) // 4, predict, 0)

    def to_owners(source, landing, sems, first_sem):
        piece = landing.shape[1]
        return [
            remote(
                source.at[rows_at(peer, piece)],
                landing.at[d],
                sems[0].at[first_sem + d],
                sems[1].at[first_sem + d],
                row,
                peer,
            )
            for d, peer in enumerate(col_peers)
        ]

    def to_all(source, landing, sems, first_sem):
        here = rows_at(col, landing.shape[1])
        return [
            remote(
                source.at[here],
                source.at[here],
                sems[0].at[first_sem + d],
                sems[1].at[first_sem + d],
                row,
                peer,
            )
            for d, peer in enumerate(col_peers)
        ]

    def add_pieces(source, landing, target):
        here = rows_at(col, landing.shape[1])
        mine = source[here]
        for d in range(n_col - 1):
            mine = mine + landing[d]
        target[here] = mine

    out_sems, back_sems = (refs.send_b, refs.recv_b), (refs.send_c, refs.recv_c)
    bins_out = to_owners(bins_sum, refs.bins_landing, out_sems, 0)
    taps_out = to_owners(taps_sum, refs.taps_landing, out_sems, n_col - 1)
    bins_back = to_all(bins_total, refs.bins_landing, back_sems, 0)
    taps_back = to_all(taps_total, refs.taps_landing, back_sems, n_col - 1)

    @pl.when(row == owner)
    def _():
        mine = col_ref[...]
        for d in range(n_row - 1):
            owned_copy(d, row_peers[0]).wait_recv()
            mine = mine + refs.from_owned[d]
        begin = lax.rem(col, ratio) * columns
        bins_sum[pl.ds(pl.multiple_of(begin, STEP), columns + 2 * STEP)] += mine

    @pl.when(row != owner)
    def _():
        owned_copy(away, owner).wait_send()

    start(bins_out)
    some(0)
    wait(to_row)
    mine = refs.packed[rows_at(row, chunk)]
    for d in range(n_row - 1):
        mine = mine + refs.from_row[d]
    taps_sum[:chunk] = mine
    start(taps_out)

    wait(bins_out)
    add_pieces(bins_sum, refs.bins_landing, bins_total)
    start(bins_back)
    some(1)
    wait(taps_out)
    add_pieces(taps_sum, refs.taps_landing, taps_total)
    start(taps_back)
    some(2)

    wait(bins_back)
    below, above = lax.rem(row + n_row - 1, n_row), lax.rem(row + 1, n_row)
    borders = [
        remote(
            bins_total.at[pl.ds(begin, STEP)],
            refs.border.at[d],
            refs.send_f.at[d],
            refs.recv_f.at[d],
            peer,
            col,
        )
        for d, (peer, begin) in enumerate([(below, 0), (above, span - STEP)])
    ]
    start(borders)
    wait(taps_back)
    here = rows_at(row, chunk)
    spread_taps = [
        remote(
            taps_total.at[pl.ds(0, chunk)],
            every.at[here],
            refs.send_d.at[d],
            refs.recv_d.at[d],
            peer,
            col,
        )
        for d, peer in enumerate(row_peers)
    ]
    start(spread_taps)
    every[here] = taps_total[:chunk]
    some(3)
    refs.bins_out[...] = bins_total[STEP : span - STEP]
    wait(borders)
    refs.bins_out[rows - STEP :] += refs.border[0]
    refs.bins_out[:STEP] += refs.border[1]
    wait(spread_taps)
    refs.taps_out[:taps] = every[:taps, :channels]
    refs.taps_out[taps:] = every[:taps, channels:]


def finish_kernel(
    bins, pred_in, taps_in, bins_in, pred_out, taps_out, bins_out, taps_ref, bins_ref, sem
):
    copies = [
        pltpu.make_async_copy(pred_in, pred_out, sem.at[0]),
        pltpu.make_async_copy(taps_ref, taps_out, sem.at[1]),
        pltpu.make_async_copy(bins_ref, bins_out, sem.at[2]),
    ]
    copies[0].start()
    taps_ref[...] = taps_in[...] / bins
    copies[1].start()
    bins_ref[...] = bins_in[...] * float(bins) ** (-0.5)
    copies[2].start()
    for copy in copies:
        copy.wait()


def in_hbm(x):
    return pltpu.with_memory_space_constraint(x, pltpu.HBM)


def round_up(value, step):
    return -(-value // step) * step


def on_device(n_row, n_col, embedding, kernel, cotangent):
    rows, columns, channels = cotangent.shape
    lanes = 2 * channels
    bins = n_row * rows
    half = columns // 2
    blocks = half // STEP
    span = rows + 2 * STEP
    depth = half + 2 * STEP
    taps = 9 * channels
    chunk = round_up(-(-taps // (2 * n_row)), STEP)
    taps_piece = round_up(-(-chunk // n_col), STEP)
    bins_piece = round_up(-(-span // n_col), STEP)
    f32, bf16 = jnp.float32, jnp.bfloat16
    dma = pltpu.SemaphoreType.DMA
    outputs = {
        "pred": jax.ShapeDtypeStruct((columns, channels, rows), f32),
        "taps_out": jax.ShapeDtypeStruct((taps, channels), f32),
        "bins_out": jax.ShapeDtypeStruct((rows, lanes), f32),
    }
    scratch = {
        "emb": pltpu.VMEM((rows, lanes), bf16),
        "kernel": pltpu.VMEM(kernel.shape, bf16),
        "cot": pltpu.VMEM((columns, channels, rows), bf16),
        "held": pltpu.VMEM((n_row - 1, rows, lanes), bf16),
        "wide": pltpu.VMEM((bins + 2 * STEP, lanes), f32),
        "weight": pltpu.VMEM((3 * lanes, 3 * lanes), bf16),
        "u_col": pltpu.VMEM((depth, lanes), f32),
        "v_col": pltpu.VMEM((depth, lanes), f32),
        "act": pltpu.VMEM((blocks + 2, STEP * span, lanes), bf16),
        "turned": pltpu.VMEM((blocks, STEP * span, 3 * lanes), bf16),
        "grad": pltpu.VMEM((blocks + 2, STEP, span, lanes), f32),
        "product": pltpu.VMEM((3 * lanes, 3 * lanes), f32),
        "u_sum": pltpu.VMEM((depth, lanes), f32),
        "v_sum": pltpu.VMEM((depth, lanes), f32),
        "flat": pltpu.VMEM((taps, channels), f32),
        "packed": pltpu.VMEM((n_row * chunk, lanes), f32),
        "col": pltpu.VMEM((columns + 2 * STEP, lanes), f32),
        "from_row": pltpu.VMEM((n_row - 1, chunk, lanes), f32),
        "from_owned": pltpu.VMEM((n_row - 1, columns + 2 * STEP, lanes), f32),
        "bins_sum": pltpu.VMEM((n_col * bins_piece, lanes), f32),
        "bins_landing": pltpu.VMEM((n_col - 1, bins_piece, lanes), f32),
        "bins_total": pltpu.VMEM((n_col * bins_piece, lanes), f32),
        "taps_sum": pltpu.VMEM((n_col * taps_piece, lanes), f32),
        "taps_landing": pltpu.VMEM((n_col - 1, taps_piece, lanes), f32),
        "taps_total": pltpu.VMEM((n_col * taps_piece, lanes), f32),
        "every": pltpu.VMEM((n_row * chunk, lanes), f32),
        "border": pltpu.VMEM((2, STEP, lanes), f32),
        "in_sem": dma((2,)),
        "cot_sem": dma((blocks, 2)),
        "send_g": dma((n_row - 1,)),
        "recv_g": dma((n_row - 1,)),
        "send_a": dma((n_row - 1,)),
        "recv_a": dma((n_row - 1,)),
        "send_b": dma((2 * (n_col - 1),)),
        "recv_b": dma((2 * (n_col - 1),)),
        "send_c": dma((2 * (n_col - 1),)),
        "recv_c": dma((2 * (n_col - 1),)),
        "send_d": dma((n_row - 1,)),
        "recv_d": dma((n_row - 1,)),
        "send_e": dma((1,)),
        "recv_e": dma((n_row - 1,)),
        "send_f": dma((2,)),
        "recv_f": dma((2,)),
    }
    names = ["emb_hbm", "kernel_hbm", "cot_hbm", *outputs, *scratch]

    def tile(*refs):
        tile_kernel(n_row, n_col, chunk, types.SimpleNamespace(**dict(zip(names, refs))))

    prediction, grad_kernel, grad_bins = pl.pallas_call(
        tile,
        out_shape=tuple(outputs.values()),
        in_specs=[HBM, HBM, HBM],
        out_specs=(VMEM, VMEM, VMEM),
        scratch_shapes=list(scratch.values()),
        compiler_params=pltpu.CompilerParams(
            collective_id=0, has_side_effects=True, vmem_limit_bytes=32 * 2**20
        ),
        name="tile_gradients",
    )(*[in_hbm(x) for x in (embedding, kernel, cotangent.transpose(1, 2, 0))])

    prediction, grad_kernel, grad_bins = pl.pallas_call(
        functools.partial(finish_kernel, bins),
        out_shape=tuple(outputs.values()),
        in_specs=[VMEM, VMEM, VMEM],
        out_specs=(HBM, HBM, HBM),
        scratch_shapes=[
            pltpu.VMEM((taps, channels), f32),
            pltpu.VMEM((rows, lanes), f32),
            dma((3,)),
        ],
        compiler_params=pltpu.CompilerParams(vmem_limit_bytes=24 * 2**20),
        name="finish",
    )(prediction, grad_kernel, grad_bins)
    return prediction.transpose(2, 0, 1), grad_kernel.reshape(kernel.shape), grad_bins


def solution(mesh):
    in_specs = (P("row", None), P(), P("row", "col", None))
    out_specs = (P("row", "col", None), P(), P("row", None))
    return jax.shard_map(
        functools.partial(on_device, mesh.shape["row"], mesh.shape["col"]),
        mesh=mesh,
        in_specs=in_specs,
        out_specs=out_specs,
        check_vma=False,
    )
```

```python
import functools
import types

import jax
import jax.numpy as jnp
from jax import lax
from jax.experimental import pallas as pl
from jax.experimental.pallas import tpu as pltpu
from jax.sharding import PartitionSpec as P

STEP = 8
MESH = pl.DeviceIdType.MESH
VMEM = pl.BlockSpec(memory_space=pltpu.VMEM)
HBM = pl.BlockSpec(memory_space=pltpu.HBM)


def signal(barrier, row, col):
    pl.semaphore_signal(barrier, inc=1, device_id=(row, col), device_id_type=MESH)


def remote(src, dst, send, recv, row, col):
    return pltpu.make_async_remote_copy(
        src_ref=src,
        dst_ref=dst,
        send_sem=send,
        recv_sem=recv,
        device_id=(row, col),
        device_id_type=MESH,
    )


def tile_kernel(n_row, n_col, chunk, refs):
    emb_hbm, kernel_hbm, cot_hbm = refs.emb_hbm, refs.kernel_hbm, refs.cot_hbm
    wide_ref, weight_ref, cot_ref, pred_ref = refs.wide, refs.weight, refs.cot, refs.pred
    act_ref, turned_ref, grad_ref, product_ref = refs.act, refs.turned, refs.grad, refs.product
    col_ref, every = refs.col, refs.every
    bins_sum, taps_sum = refs.bins_sum, refs.taps_sum
    bins_total, taps_total = refs.bins_total, refs.taps_total
    columns, channels, rows = cot_ref.shape
    half = columns // 2
    blocks = half // STEP
    span = rows + 2 * STEP
    depth = half + 2 * STEP
    lanes = 2 * channels
    bins = n_row * rows
    ratio = rows // columns
    row, col = lax.axis_index("row"), lax.axis_index("col")
    row0, col0 = row * rows, col * columns
    owner = col // ratio
    row_peers = [lax.rem(row + d, n_row) for d in range(1, n_row)]
    col_peers = [lax.rem(col + d, n_col) for d in range(1, n_col)]

    def local(source, target, sem):
        return pltpu.make_async_copy(source, target, sem)

    def cot_copy(n, h):
        at = pl.ds(h * half + n * STEP, STEP)
        return local(cot_hbm.at[at], cot_ref.at[at], refs.cot_sem.at[n, h])

    def rows_at(index, count):
        return pl.ds(pl.multiple_of(index * count, STEP), count)

    def start(copies):
        for copy in copies:
            copy.start()

    def wait(copies):
        for copy in copies:
            copy.wait()

    barrier = pltpu.get_barrier_semaphore()
    for peer in row_peers:
        signal(barrier, peer, col)
    for peer in col_peers:
        signal(barrier, row, peer)
    inputs = [
        local(emb_hbm, refs.emb, refs.in_sem.at[0]),
        local(kernel_hbm, refs.kernel, refs.in_sem.at[1]),
    ]
    start(inputs)
    start([cot_copy(n, h) for n in range(blocks) for h in range(2)])

    grad_ref[...] = jnp.zeros_like(grad_ref)
    product_ref[...] = jnp.zeros_like(product_ref)
    zeros = jnp.zeros((STEP, lanes), jnp.float32)
    wide_ref[:STEP] = zeros
    wide_ref[STEP + bins :] = zeros
    for ref, used in [(bins_sum, rows), (taps_sum, chunk + 2 * STEP)]:
        if ref.shape[0] > used:
            ref[used:] = jnp.zeros((ref.shape[0] - used, lanes), jnp.float32)

    wait(inputs)
    pl.semaphore_wait(barrier, n_row + n_col - 2)
    gather = [
        remote(refs.emb, refs.held.at[d], refs.send_g.at[d], refs.recv_g.at[d], peer, col)
        for d, peer in enumerate(row_peers)
    ]
    start(gather)

    none = jnp.zeros((channels, channels), jnp.float32)
    for a in range(3):
        for b in range(3):
            w = refs.kernel[a, b].astype(jnp.float32)
            both = jnp.concatenate(
                [jnp.concatenate([w, none], axis=1), jnp.concatenate([none, w], axis=1)], axis=0
            )
            weight_ref[b * lanes : (b + 1) * lanes, a * lanes : (a + 1) * lanes] = both.astype(
                jnp.bfloat16
            )

    def spread(n, carry):
        wait([cot_copy(n, h) for h in range(2)])
        cot = []
        for k in range(STEP):
            at = n * STEP + k
            stack = jnp.concatenate([cot_ref[at], cot_ref[half + at]], axis=0)
            cot.append(stack.astype(jnp.float32).T)
        cot = jnp.stack(cot)
        zero = jnp.zeros((STEP, STEP, lanes), jnp.float32)
        shifted = [
            jnp.concatenate([zero] * a + [cot] + [zero] * (2 - a), axis=1).astype(jnp.bfloat16)
            for a in range(3)
        ]
        y = jnp.concatenate(shifted, axis=2).reshape(STEP * span, 3 * lanes)
        turned_ref[n] = y
        back = lax.dot_general(
            y, weight_ref[...], (((1,), (1,)), ((), ())), preferred_element_type=jnp.float32
        ).reshape(STEP, span, 3 * lanes)
        for b in range(3):
            grad_ref[n + b] += back[:, :, b * lanes : (b + 1) * lanes]
        return carry

    lax.fori_loop(0, blocks, spread, 0)

    wide_ref[pl.ds(pl.multiple_of(STEP + row0, STEP), rows)] = refs.emb[...].astype(jnp.float32)
    for d, copy in enumerate(gather):
        copy.wait()
        peer = lax.rem(row + n_row - 1 - d, n_row)
        at = pl.ds(pl.multiple_of(STEP + peer * rows, STEP), rows)
        wide_ref[at] = refs.held[d].astype(jnp.float32)

    def first(shape):
        return lax.broadcasted_iota(jnp.int32, shape, len(shape) - 1) < channels

    def swap(x):
        return pltpu.roll(x, channels, 1)

    low = wide_ref[pl.ds(pl.multiple_of(col0, STEP), depth)]
    high = wide_ref[pl.ds(pl.multiple_of(col0 + half, STEP), depth)]
    in_first = first((depth, lanes))
    refs.u_col[...] = jnp.where(in_first, low, swap(high))
    refs.v_col[...] = jnp.where(in_first, swap(low), high)
    side = wide_ref[pl.ds(pl.multiple_of(row0, STEP), span)]
    in_first_row = first((span, lanes))
    u_row = jnp.where(in_first_row, side, swap(side))
    v_row = jnp.where(in_first_row, swap(side), side)
    row_pos = row0 - STEP + lax.broadcasted_iota(jnp.int32, (span, lanes), 0)
    row_in = jnp.where((row_pos >= 0) & (row_pos < bins), 1.0, 0.0)

    def activate(m, carry):
        u_total, v_total = carry
        at = pl.ds(pl.multiple_of(m * STEP, STEP), STEP)
        shape = (STEP, 1, lanes)
        pos = col0 - STEP + m * STEP + lax.broadcasted_iota(jnp.int32, shape, 0)
        pos = pos + jnp.where(first(shape), 0, half)
        col_in = jnp.where((pos >= 0) & (pos < bins), 1.0, 0.0)
        u_col = refs.u_col[at][:, None, :]
        pairs = u_col * u_row[None] + refs.v_col[at][:, None, :] + v_row[None]
        s = 0.5 * jnp.tanh(0.5 * pairs) + 0.5
        s = s * (col_in * row_in[None])
        act = pairs * s
        act_ref[m] = act.reshape(STEP * span, lanes).astype(jnp.bfloat16)
        grad = grad_ref[m] * (s + act * (1.0 - s))
        refs.u_sum[at] = jnp.sum(grad * u_row[None], axis=1)
        refs.v_sum[at] = jnp.sum(grad, axis=1)
        u_total = u_total + jnp.sum(grad * u_col, axis=0)
        return u_total, v_total + jnp.sum(grad, axis=0)

    nothing = jnp.zeros((span, lanes), jnp.float32)
    u_total, v_total = lax.fori_loop(0, blocks + 2, activate, (nothing, nothing))

    row_part = jnp.where(in_first_row, u_total + swap(u_total), v_total + swap(v_total))
    refs.row[...] = row_part
    u_sum, v_sum = refs.u_sum[...], refs.v_sum[...]
    col_ref[:depth] = jnp.where(in_first, u_sum, swap(v_sum))
    col_ref[depth:] = jnp.zeros((half, lanes), jnp.float32)
    col_ref[half:] += jnp.where(in_first, swap(u_sum), v_sum)

    away = lax.rem(owner + n_row - row, n_row) - 1

    def owned_copy(d, target):
        return remote(
            col_ref, refs.from_owned.at[d], refs.send_e.at[0], refs.recv_e.at[d], target, col
        )

    @pl.when(row != owner)
    def _():
        owned_copy(away, owner).start()

    def lay(n):
        return jnp.concatenate([act_ref[n + b] for b in range(3)], axis=1)

    def multiply(n, carry):
        product_ref[...] += lax.dot_general(
            lay(n), turned_ref[n], (((0,), (0,)), ((), ())), preferred_element_type=jnp.float32
        )
        return carry

    lax.fori_loop(0, blocks, multiply, 0)
    for a in range(3):
        for b in range(3):
            block = product_ref[b * lanes : (b + 1) * lanes, a * lanes : (a + 1) * lanes]
            tap = (3 * a + b) * channels
            refs.flat[tap : tap + channels] = (
                block[:channels, :channels] + block[channels:, channels:]
            )
    taps = 9 * channels // 2
    refs.packed[:taps] = jnp.concatenate([refs.flat[:taps], refs.flat[taps:]], axis=1)
    if n_row * chunk > taps:
        refs.packed[taps:] = jnp.zeros((n_row * chunk - taps, lanes), jnp.float32)
    to_row = [
        remote(
            refs.packed.at[rows_at(peer, chunk)],
            refs.from_row.at[d],
            refs.send_a.at[d],
            refs.recv_a.at[d],
            peer,
            col,
        )
        for d, peer in enumerate(row_peers)
    ]
    start(to_row)

    def predict(n, carry):
        out = jnp.dot(lay(n), weight_ref[...], preferred_element_type=jnp.float32)
        out = out.reshape(STEP, span, 3 * lanes)
        out = (
            out[:, :rows, :lanes]
            + out[:, STEP : STEP + rows, lanes : 2 * lanes]
            + out[:, 2 * STEP :, 2 * lanes :]
        )
        for k in range(STEP):
            at = n * STEP + k
            turned = out[k].T
            pred_ref[at] = turned[:channels]
            pred_ref[half + at] = turned[channels:]
        return carry

    def some(part):
        lax.fori_loop(blocks * part // 4, blocks * (part + 1) // 4, predict, 0)

    def to_owners(source, landing, sems, first_sem):
        piece = landing.shape[1]
        return [
            remote(
                source.at[rows_at(peer, piece)],
                landing.at[d],
                sems[0].at[first_sem + d],
                sems[1].at[first_sem + d],
                row,
                peer,
            )
            for d, peer in enumerate(col_peers)
        ]

    def to_all(source, landing, sems, first_sem):
        here = rows_at(col, landing.shape[1])
        return [
            remote(
                source.at[here],
                source.at[here],
                sems[0].at[first_sem + d],
                sems[1].at[first_sem + d],
                row,
                peer,
            )
            for d, peer in enumerate(col_peers)
        ]

    def add_pieces(source, landing, target):
        here = rows_at(col, landing.shape[1])
        mine = source[here]
        for d in range(n_col - 1):
            mine = mine + landing[d]
        target[here] = mine

    out_sems, back_sems = (refs.send_b, refs.recv_b), (refs.send_c, refs.recv_c)
    bins_out = to_owners(bins_sum, refs.bins_landing, out_sems, 0)
    taps_out = to_owners(taps_sum, refs.taps_landing, out_sems, n_col - 1)
    bins_back = to_all(bins_total, refs.bins_landing, back_sems, 0)
    taps_back = to_all(taps_total, refs.taps_landing, back_sems, n_col - 1)

    @pl.when(row == owner)
    def _():
        mine = col_ref[...]
        for d in range(n_row - 1):
            owned_copy(d, row_peers[0]).wait_recv()
            mine = mine + refs.from_owned[d]
        begin = lax.rem(col, ratio) * columns
        refs.row[pl.ds(pl.multiple_of(begin, STEP), columns + 2 * STEP)] += mine

    @pl.when(row != owner)
    def _():
        owned_copy(away, owner).wait_send()

    bins_sum[:rows] = refs.row[STEP : STEP + rows]
    taps_sum[chunk : chunk + STEP] = refs.row[:STEP]
    taps_sum[chunk + STEP : chunk + 2 * STEP] = refs.row[STEP + rows :]
    start(bins_out)
    some(0)
    wait(to_row)
    mine = refs.packed[rows_at(row, chunk)]
    for d in range(n_row - 1):
        mine = mine + refs.from_row[d]
    taps_sum[:chunk] = mine
    start(taps_out)

    wait(bins_out)
    add_pieces(bins_sum, refs.bins_landing, bins_total)
    start(bins_back)
    some(1)
    wait(taps_out)
    add_pieces(taps_sum, refs.taps_landing, taps_total)
    start(taps_back)
    some(2)

    wait(taps_back)
    below, above = lax.rem(row + n_row - 1, n_row), lax.rem(row + 1, n_row)
    borders = [
        remote(
            taps_total.at[pl.ds(chunk + d * STEP, STEP)],
            refs.border.at[d],
            refs.send_f.at[d],
            refs.recv_f.at[d],
            peer,
            col,
        )
        for d, peer in enumerate([below, above])
    ]
    start(borders)
    here = rows_at(row, chunk)
    spread_taps = [
        remote(
            taps_total.at[pl.ds(0, chunk)],
            every.at[here],
            refs.send_d.at[d],
            refs.recv_d.at[d],
            peer,
            col,
        )
        for d, peer in enumerate(row_peers)
    ]
    start(spread_taps)
    every[here] = taps_total[:chunk]
    some(3)
    wait(bins_back)
    refs.bins_out[...] = bins_total[:rows]
    wait(borders)
    refs.bins_out[rows - STEP :] += refs.border[0]
    refs.bins_out[:STEP] += refs.border[1]
    wait(spread_taps)
    refs.taps_out[:taps] = every[:taps, :channels]
    refs.taps_out[taps:] = every[:taps, channels:]


def finish_kernel(
    bins, pred_in, taps_in, bins_in, pred_out, taps_out, bins_out, taps_ref, bins_ref, sem
):
    copies = [
        pltpu.make_async_copy(pred_in, pred_out, sem.at[0]),
        pltpu.make_async_copy(taps_ref, taps_out, sem.at[1]),
        pltpu.make_async_copy(bins_ref, bins_out, sem.at[2]),
    ]
    copies[0].start()
    taps_ref[...] = taps_in[...] / bins
    copies[1].start()
    bins_ref[...] = bins_in[...] * float(bins) ** (-0.5)
    copies[2].start()
    for copy in copies:
        copy.wait()


def in_hbm(x):
    return pltpu.with_memory_space_constraint(x, pltpu.HBM)


def round_up(value, step):
    return -(-value // step) * step


def on_device(n_row, n_col, embedding, kernel, cotangent):
    rows, columns, channels = cotangent.shape
    lanes = 2 * channels
    bins = n_row * rows
    half = columns // 2
    blocks = half // STEP
    span = rows + 2 * STEP
    depth = half + 2 * STEP
    taps = 9 * channels
    chunk = round_up(-(-taps // (2 * n_row)), STEP)
    taps_piece = round_up(-(-(chunk + 2 * STEP) // n_col), STEP)
    bins_piece = round_up(-(-rows // n_col), STEP)
    f32, bf16 = jnp.float32, jnp.bfloat16
    dma = pltpu.SemaphoreType.DMA
    outputs = {
        "pred": jax.ShapeDtypeStruct((columns, channels, rows), f32),
        "taps_out": jax.ShapeDtypeStruct((taps, channels), f32),
        "bins_out": jax.ShapeDtypeStruct((rows, lanes), f32),
    }
    scratch = {
        "emb": pltpu.VMEM((rows, lanes), bf16),
        "kernel": pltpu.VMEM(kernel.shape, bf16),
        "cot": pltpu.VMEM((columns, channels, rows), bf16),
        "held": pltpu.VMEM((n_row - 1, rows, lanes), bf16),
        "wide": pltpu.VMEM((bins + 2 * STEP, lanes), f32),
        "weight": pltpu.VMEM((3 * lanes, 3 * lanes), bf16),
        "u_col": pltpu.VMEM((depth, lanes), f32),
        "v_col": pltpu.VMEM((depth, lanes), f32),
        "act": pltpu.VMEM((blocks + 2, STEP * span, lanes), bf16),
        "turned": pltpu.VMEM((blocks, STEP * span, 3 * lanes), bf16),
        "grad": pltpu.VMEM((blocks + 2, STEP, span, lanes), f32),
        "product": pltpu.VMEM((3 * lanes, 3 * lanes), f32),
        "u_sum": pltpu.VMEM((depth, lanes), f32),
        "v_sum": pltpu.VMEM((depth, lanes), f32),
        "flat": pltpu.VMEM((taps, channels), f32),
        "packed": pltpu.VMEM((n_row * chunk, lanes), f32),
        "col": pltpu.VMEM((columns + 2 * STEP, lanes), f32),
        "from_row": pltpu.VMEM((n_row - 1, chunk, lanes), f32),
        "from_owned": pltpu.VMEM((n_row - 1, columns + 2 * STEP, lanes), f32),
        "row": pltpu.VMEM((span, lanes), f32),
        "bins_sum": pltpu.VMEM((n_col * bins_piece, lanes), f32),
        "bins_landing": pltpu.VMEM((n_col - 1, bins_piece, lanes), f32),
        "bins_total": pltpu.VMEM((n_col * bins_piece, lanes), f32),
        "taps_sum": pltpu.VMEM((n_col * taps_piece, lanes), f32),
        "taps_landing": pltpu.VMEM((n_col - 1, taps_piece, lanes), f32),
        "taps_total": pltpu.VMEM((n_col * taps_piece, lanes), f32),
        "every": pltpu.VMEM((n_row * chunk, lanes), f32),
        "border": pltpu.VMEM((2, STEP, lanes), f32),
        "in_sem": dma((2,)),
        "cot_sem": dma((blocks, 2)),
        "send_g": dma((n_row - 1,)),
        "recv_g": dma((n_row - 1,)),
        "send_a": dma((n_row - 1,)),
        "recv_a": dma((n_row - 1,)),
        "send_b": dma((2 * (n_col - 1),)),
        "recv_b": dma((2 * (n_col - 1),)),
        "send_c": dma((2 * (n_col - 1),)),
        "recv_c": dma((2 * (n_col - 1),)),
        "send_d": dma((n_row - 1,)),
        "recv_d": dma((n_row - 1,)),
        "send_e": dma((1,)),
        "recv_e": dma((n_row - 1,)),
        "send_f": dma((2,)),
        "recv_f": dma((2,)),
    }
    names = ["emb_hbm", "kernel_hbm", "cot_hbm", *outputs, *scratch]

    def tile(*refs):
        tile_kernel(n_row, n_col, chunk, types.SimpleNamespace(**dict(zip(names, refs))))

    prediction, grad_kernel, grad_bins = pl.pallas_call(
        tile,
        out_shape=tuple(outputs.values()),
        in_specs=[HBM, HBM, HBM],
        out_specs=(VMEM, VMEM, VMEM),
        scratch_shapes=list(scratch.values()),
        compiler_params=pltpu.CompilerParams(
            collective_id=0, has_side_effects=True, vmem_limit_bytes=32 * 2**20
        ),
        name="tile_gradients",
    )(*[in_hbm(x) for x in (embedding, kernel, cotangent.transpose(1, 2, 0))])

    prediction, grad_kernel, grad_bins = pl.pallas_call(
        functools.partial(finish_kernel, bins),
        out_shape=tuple(outputs.values()),
        in_specs=[VMEM, VMEM, VMEM],
        out_specs=(HBM, HBM, HBM),
        scratch_shapes=[
            pltpu.VMEM((taps, channels), f32),
            pltpu.VMEM((rows, lanes), f32),
            dma((3,)),
        ],
        compiler_params=pltpu.CompilerParams(vmem_limit_bytes=24 * 2**20),
        name="finish",
    )(prediction, grad_kernel, grad_bins)
    return prediction.transpose(2, 0, 1), grad_kernel.reshape(kernel.shape), grad_bins


def solution(mesh):
    in_specs = (P("row", None), P(), P("row", "col", None))
    out_specs = (P("row", "col", None), P(), P("row", None))
    return jax.shard_map(
        functools.partial(on_device, mesh.shape["row"], mesh.shape["col"]),
        mesh=mesh,
        in_specs=in_specs,
        out_specs=out_specs,
        check_vma=False,
    )
```

```python
import functools
import types

import jax
import jax.numpy as jnp
from jax import lax
from jax.experimental import pallas as pl
from jax.experimental.pallas import tpu as pltpu
from jax.sharding import PartitionSpec as P

STEP = 8
MESH = pl.DeviceIdType.MESH
VMEM = pl.BlockSpec(memory_space=pltpu.VMEM)
HBM = pl.BlockSpec(memory_space=pltpu.HBM)


def signal(barrier, row, col):
    pl.semaphore_signal(barrier, inc=1, device_id=(row, col), device_id_type=MESH)


def remote(src, dst, send, recv, row, col):
    return pltpu.make_async_remote_copy(
        src_ref=src,
        dst_ref=dst,
        send_sem=send,
        recv_sem=recv,
        device_id=(row, col),
        device_id_type=MESH,
    )


def tile_kernel(n_row, n_col, chunk, refs):
    emb_hbm, kernel_hbm, cot_hbm = refs.emb_hbm, refs.kernel_hbm, refs.cot_hbm
    wide_ref, weight_ref, cot_ref, pred_ref = refs.wide, refs.weight, refs.cot, refs.pred
    act_ref, turned_ref, grad_ref, product_ref = refs.act, refs.turned, refs.grad, refs.product
    col_ref, every = refs.col, refs.every
    bins_sum, taps_sum = refs.bins_sum, refs.taps_sum
    bins_total, taps_total = refs.bins_total, refs.taps_total
    columns, channels, rows = cot_ref.shape
    half = columns // 2
    blocks = half // STEP
    span = rows + 2 * STEP
    depth = half + 2 * STEP
    lanes = 2 * channels
    bins = n_row * rows
    ratio = rows // columns
    row, col = lax.axis_index("row"), lax.axis_index("col")
    row0, col0 = row * rows, col * columns
    owner = col // ratio
    row_peers = [lax.rem(row + d, n_row) for d in range(1, n_row)]
    col_peers = [lax.rem(col + d, n_col) for d in range(1, n_col)]

    def local(source, target, sem):
        return pltpu.make_async_copy(source, target, sem)

    def cot_copy(n, h):
        at = pl.ds(h * half + n * STEP, STEP)
        return local(cot_hbm.at[at], cot_ref.at[at], refs.cot_sem.at[n, h])

    def rows_at(index, count):
        return pl.ds(pl.multiple_of(index * count, STEP), count)

    def start(copies):
        for copy in copies:
            copy.start()

    def wait(copies):
        for copy in copies:
            copy.wait()

    barrier = pltpu.get_barrier_semaphore()
    for peer in row_peers:
        signal(barrier, peer, col)
    for peer in col_peers:
        signal(barrier, row, peer)
    inputs = [
        local(emb_hbm, refs.emb, refs.in_sem.at[0]),
        local(kernel_hbm, refs.kernel, refs.in_sem.at[1]),
    ]
    start(inputs)
    start([cot_copy(n, h) for n in range(blocks) for h in range(2)])

    grad_ref[...] = jnp.zeros_like(grad_ref)
    product_ref[...] = jnp.zeros_like(product_ref)
    zeros = jnp.zeros((STEP, lanes), jnp.float32)
    wide_ref[:STEP] = zeros
    wide_ref[STEP + bins :] = zeros
    for ref, used in [(bins_sum, rows), (taps_sum, chunk + 2 * STEP)]:
        if ref.shape[0] > used:
            ref[used:] = jnp.zeros((ref.shape[0] - used, lanes), jnp.float32)

    wait(inputs)
    pl.semaphore_wait(barrier, n_row + n_col - 2)
    gather = [
        remote(refs.emb, refs.held.at[d], refs.send_g.at[d], refs.recv_g.at[d], peer, col)
        for d, peer in enumerate(row_peers)
    ]
    start(gather)

    none = jnp.zeros((channels, channels), jnp.float32)
    for a in range(3):
        for b in range(3):
            w = refs.kernel[a, b].astype(jnp.float32)
            both = jnp.concatenate(
                [jnp.concatenate([w, none], axis=1), jnp.concatenate([none, w], axis=1)], axis=0
            )
            weight_ref[b * lanes : (b + 1) * lanes, a * lanes : (a + 1) * lanes] = both.astype(
                jnp.bfloat16
            )

    def spread(n, carry):
        wait([cot_copy(n, h) for h in range(2)])
        cot = []
        for k in range(STEP):
            at = n * STEP + k
            stack = jnp.concatenate([cot_ref[at], cot_ref[half + at]], axis=0)
            cot.append(stack.astype(jnp.float32).T)
        cot = jnp.stack(cot)
        zero = jnp.zeros((STEP, STEP, lanes), jnp.float32)
        shifted = [
            jnp.concatenate([zero] * a + [cot] + [zero] * (2 - a), axis=1).astype(jnp.bfloat16)
            for a in range(3)
        ]
        y = jnp.concatenate(shifted, axis=2).reshape(STEP * span, 3 * lanes)
        turned_ref[n] = y
        back = lax.dot_general(
            y, weight_ref[...], (((1,), (1,)), ((), ())), preferred_element_type=jnp.float32
        ).reshape(STEP, span, 3 * lanes)
        for b in range(3):
            grad_ref[n + b] += back[:, :, b * lanes : (b + 1) * lanes]
        return carry

    lax.fori_loop(0, blocks, spread, 0)

    wide_ref[pl.ds(pl.multiple_of(STEP + row0, STEP), rows)] = refs.emb[...].astype(jnp.float32)
    for d, copy in enumerate(gather):
        copy.wait()
        peer = lax.rem(row + n_row - 1 - d, n_row)
        at = pl.ds(pl.multiple_of(STEP + peer * rows, STEP), rows)
        wide_ref[at] = refs.held[d].astype(jnp.float32)

    def first(shape):
        return lax.broadcasted_iota(jnp.int32, shape, len(shape) - 1) < channels

    def swap(x):
        return pltpu.roll(x, channels, 1)

    low = wide_ref[pl.ds(pl.multiple_of(col0, STEP), depth)]
    high = wide_ref[pl.ds(pl.multiple_of(col0 + half, STEP), depth)]
    in_first = first((depth, lanes))
    refs.u_col[...] = jnp.where(in_first, low, swap(high))
    refs.v_col[...] = jnp.where(in_first, swap(low), high)
    side = wide_ref[pl.ds(pl.multiple_of(row0, STEP), span)]
    in_first_row = first((span, lanes))
    u_row = jnp.where(in_first_row, side, swap(side))
    v_row = jnp.where(in_first_row, swap(side), side)
    row_pos = row0 - STEP + lax.broadcasted_iota(jnp.int32, (span, lanes), 0)
    row_in = jnp.where((row_pos >= 0) & (row_pos < bins), 1.0, 0.0)

    def activate(m, carry):
        at = pl.ds(pl.multiple_of(m * STEP, STEP), STEP)
        shape = (STEP, 1, lanes)
        pos = col0 - STEP + m * STEP + lax.broadcasted_iota(jnp.int32, shape, 0)
        pos = pos + jnp.where(first(shape), 0, half)
        col_in = jnp.where((pos >= 0) & (pos < bins), 1.0, 0.0)
        u_col = refs.u_col[at][:, None, :]
        pairs = u_col * u_row[None] + refs.v_col[at][:, None, :] + v_row[None]
        s = 0.5 * jnp.tanh(0.5 * pairs) + 0.5
        s = s * (col_in * row_in[None])
        act = pairs * s
        act_ref[m] = act.reshape(STEP * span, lanes).astype(jnp.bfloat16)
        refs.slope[m] = s + act * (1.0 - s)
        return carry

    lax.fori_loop(0, blocks + 2, activate, 0)

    def lay(n):
        return jnp.concatenate([act_ref[n + b] for b in range(3)], axis=1)

    def multiply(n, carry):
        product_ref[...] += lax.dot_general(
            lay(n), turned_ref[n], (((0,), (0,)), ((), ())), preferred_element_type=jnp.float32
        )
        return carry

    lax.fori_loop(0, blocks, multiply, 0)
    for a in range(3):
        for b in range(3):
            block = product_ref[b * lanes : (b + 1) * lanes, a * lanes : (a + 1) * lanes]
            tap = (3 * a + b) * channels
            refs.flat[tap : tap + channels] = (
                block[:channels, :channels] + block[channels:, channels:]
            )
    taps = 9 * channels // 2
    refs.packed[:taps] = jnp.concatenate([refs.flat[:taps], refs.flat[taps:]], axis=1)
    if n_row * chunk > taps:
        refs.packed[taps:] = jnp.zeros((n_row * chunk - taps, lanes), jnp.float32)
    to_row = [
        remote(
            refs.packed.at[rows_at(peer, chunk)],
            refs.from_row.at[d],
            refs.send_a.at[d],
            refs.recv_a.at[d],
            peer,
            col,
        )
        for d, peer in enumerate(row_peers)
    ]
    start(to_row)

    def reduce(m, carry):
        u_total, v_total = carry
        at = pl.ds(pl.multiple_of(m * STEP, STEP), STEP)
        grad = grad_ref[m] * refs.slope[m]
        refs.u_sum[at] = jnp.sum(grad * u_row[None], axis=1)
        refs.v_sum[at] = jnp.sum(grad, axis=1)
        u_total = u_total + jnp.sum(grad * refs.u_col[at][:, None, :], axis=0)
        return u_total, v_total + jnp.sum(grad, axis=0)

    nothing = jnp.zeros((span, lanes), jnp.float32)
    u_total, v_total = lax.fori_loop(0, blocks + 2, reduce, (nothing, nothing))

    row_part = jnp.where(in_first_row, u_total + swap(u_total), v_total + swap(v_total))
    refs.row[...] = row_part
    u_sum, v_sum = refs.u_sum[...], refs.v_sum[...]
    col_ref[:depth] = jnp.where(in_first, u_sum, swap(v_sum))
    col_ref[depth:] = jnp.zeros((half, lanes), jnp.float32)
    col_ref[half:] += jnp.where(in_first, swap(u_sum), v_sum)

    away = lax.rem(owner + n_row - row, n_row) - 1

    def owned_copy(d, target):
        return remote(
            col_ref, refs.from_owned.at[d], refs.send_e.at[0], refs.recv_e.at[d], target, col
        )

    @pl.when(row != owner)
    def _():
        owned_copy(away, owner).start()

    def predict(n, carry):
        out = jnp.dot(lay(n), weight_ref[...], preferred_element_type=jnp.float32)
        out = out.reshape(STEP, span, 3 * lanes)
        out = (
            out[:, :rows, :lanes]
            + out[:, STEP : STEP + rows, lanes : 2 * lanes]
            + out[:, 2 * STEP :, 2 * lanes :]
        )
        for k in range(STEP):
            at = n * STEP + k
            turned = out[k].T
            pred_ref[at] = turned[:channels]
            pred_ref[half + at] = turned[channels:]
        return carry

    def some(part):
        lax.fori_loop(blocks * part // 4, blocks * (part + 1) // 4, predict, 0)

    def to_owners(source, landing, sems, first_sem):
        piece = landing.shape[1]
        return [
            remote(
                source.at[rows_at(peer, piece)],
                landing.at[d],
                sems[0].at[first_sem + d],
                sems[1].at[first_sem + d],
                row,
                peer,
            )
            for d, peer in enumerate(col_peers)
        ]

    def to_all(source, landing, sems, first_sem):
        here = rows_at(col, landing.shape[1])
        return [
            remote(
                source.at[here],
                source.at[here],
                sems[0].at[first_sem + d],
                sems[1].at[first_sem + d],
                row,
                peer,
            )
            for d, peer in enumerate(col_peers)
        ]

    def add_pieces(source, landing, target):
        here = rows_at(col, landing.shape[1])
        mine = source[here]
        for d in range(n_col - 1):
            mine = mine + landing[d]
        target[here] = mine

    out_sems, back_sems = (refs.send_b, refs.recv_b), (refs.send_c, refs.recv_c)
    bins_out = to_owners(bins_sum, refs.bins_landing, out_sems, 0)
    taps_out = to_owners(taps_sum, refs.taps_landing, out_sems, n_col - 1)
    bins_back = to_all(bins_total, refs.bins_landing, back_sems, 0)
    taps_back = to_all(taps_total, refs.taps_landing, back_sems, n_col - 1)

    some(0)

    @pl.when(row == owner)
    def _():
        mine = col_ref[...]
        for d in range(n_row - 1):
            owned_copy(d, row_peers[0]).wait_recv()
            mine = mine + refs.from_owned[d]
        begin = lax.rem(col, ratio) * columns
        refs.row[pl.ds(pl.multiple_of(begin, STEP), columns + 2 * STEP)] += mine

    @pl.when(row != owner)
    def _():
        owned_copy(away, owner).wait_send()

    bins_sum[:rows] = refs.row[STEP : STEP + rows]
    taps_sum[chunk : chunk + STEP] = refs.row[:STEP]
    taps_sum[chunk + STEP : chunk + 2 * STEP] = refs.row[STEP + rows :]
    start(bins_out)
    wait(to_row)
    mine = refs.packed[rows_at(row, chunk)]
    for d in range(n_row - 1):
        mine = mine + refs.from_row[d]
    taps_sum[:chunk] = mine
    start(taps_out)

    wait(bins_out)
    add_pieces(bins_sum, refs.bins_landing, bins_total)
    start(bins_back)
    some(1)
    wait(taps_out)
    add_pieces(taps_sum, refs.taps_landing, taps_total)
    start(taps_back)
    some(2)

    wait(taps_back)
    below, above = lax.rem(row + n_row - 1, n_row), lax.rem(row + 1, n_row)
    borders = [
        remote(
            taps_total.at[pl.ds(chunk + d * STEP, STEP)],
            refs.border.at[d],
            refs.send_f.at[d],
            refs.recv_f.at[d],
            peer,
            col,
        )
        for d, peer in enumerate([below, above])
    ]
    start(borders)
    here = rows_at(row, chunk)
    spread_taps = [
        remote(
            taps_total.at[pl.ds(0, chunk)],
            every.at[here],
            refs.send_d.at[d],
            refs.recv_d.at[d],
            peer,
            col,
        )
        for d, peer in enumerate(row_peers)
    ]
    start(spread_taps)
    every[here] = taps_total[:chunk]
    some(3)
    wait(bins_back)
    refs.bins_out[...] = bins_total[:rows]
    wait(borders)
    refs.bins_out[rows - STEP :] += refs.border[0]
    refs.bins_out[:STEP] += refs.border[1]
    wait(spread_taps)
    refs.taps_out[:taps] = every[:taps, :channels]
    refs.taps_out[taps:] = every[:taps, channels:]


def finish_kernel(
    bins, pred_in, taps_in, bins_in, pred_out, taps_out, bins_out, taps_ref, bins_ref, sem
):
    copies = [
        pltpu.make_async_copy(pred_in, pred_out, sem.at[0]),
        pltpu.make_async_copy(taps_ref, taps_out, sem.at[1]),
        pltpu.make_async_copy(bins_ref, bins_out, sem.at[2]),
    ]
    copies[0].start()
    taps_ref[...] = taps_in[...] / bins
    copies[1].start()
    bins_ref[...] = bins_in[...] * float(bins) ** (-0.5)
    copies[2].start()
    for copy in copies:
        copy.wait()


def in_hbm(x):
    return pltpu.with_memory_space_constraint(x, pltpu.HBM)


def round_up(value, step):
    return -(-value // step) * step


def on_device(n_row, n_col, embedding, kernel, cotangent):
    rows, columns, channels = cotangent.shape
    lanes = 2 * channels
    bins = n_row * rows
    half = columns // 2
    blocks = half // STEP
    span = rows + 2 * STEP
    depth = half + 2 * STEP
    taps = 9 * channels
    chunk = round_up(-(-taps // (2 * n_row)), STEP)
    taps_piece = round_up(-(-(chunk + 2 * STEP) // n_col), STEP)
    bins_piece = round_up(-(-rows // n_col), STEP)
    f32, bf16 = jnp.float32, jnp.bfloat16
    dma = pltpu.SemaphoreType.DMA
    outputs = {
        "pred": jax.ShapeDtypeStruct((columns, channels, rows), f32),
        "taps_out": jax.ShapeDtypeStruct((taps, channels), f32),
        "bins_out": jax.ShapeDtypeStruct((rows, lanes), f32),
    }
    scratch = {
        "emb": pltpu.VMEM((rows, lanes), bf16),
        "kernel": pltpu.VMEM(kernel.shape, bf16),
        "cot": pltpu.VMEM((columns, channels, rows), bf16),
        "held": pltpu.VMEM((n_row - 1, rows, lanes), bf16),
        "wide": pltpu.VMEM((bins + 2 * STEP, lanes), f32),
        "weight": pltpu.VMEM((3 * lanes, 3 * lanes), bf16),
        "u_col": pltpu.VMEM((depth, lanes), f32),
        "v_col": pltpu.VMEM((depth, lanes), f32),
        "act": pltpu.VMEM((blocks + 2, STEP * span, lanes), bf16),
        "turned": pltpu.VMEM((blocks, STEP * span, 3 * lanes), bf16),
        "grad": pltpu.VMEM((blocks + 2, STEP, span, lanes), f32),
        "slope": pltpu.VMEM((blocks + 2, STEP, span, lanes), f32),
        "product": pltpu.VMEM((3 * lanes, 3 * lanes), f32),
        "u_sum": pltpu.VMEM((depth, lanes), f32),
        "v_sum": pltpu.VMEM((depth, lanes), f32),
        "flat": pltpu.VMEM((taps, channels), f32),
        "packed": pltpu.VMEM((n_row * chunk, lanes), f32),
        "col": pltpu.VMEM((columns + 2 * STEP, lanes), f32),
        "from_row": pltpu.VMEM((n_row - 1, chunk, lanes), f32),
        "from_owned": pltpu.VMEM((n_row - 1, columns + 2 * STEP, lanes), f32),
        "row": pltpu.VMEM((span, lanes), f32),
        "bins_sum": pltpu.VMEM((n_col * bins_piece, lanes), f32),
        "bins_landing": pltpu.VMEM((n_col - 1, bins_piece, lanes), f32),
        "bins_total": pltpu.VMEM((n_col * bins_piece, lanes), f32),
        "taps_sum": pltpu.VMEM((n_col * taps_piece, lanes), f32),
        "taps_landing": pltpu.VMEM((n_col - 1, taps_piece, lanes), f32),
        "taps_total": pltpu.VMEM((n_col * taps_piece, lanes), f32),
        "every": pltpu.VMEM((n_row * chunk, lanes), f32),
        "border": pltpu.VMEM((2, STEP, lanes), f32),
        "in_sem": dma((2,)),
        "cot_sem": dma((blocks, 2)),
        "send_g": dma((n_row - 1,)),
        "recv_g": dma((n_row - 1,)),
        "send_a": dma((n_row - 1,)),
        "recv_a": dma((n_row - 1,)),
        "send_b": dma((2 * (n_col - 1),)),
        "recv_b": dma((2 * (n_col - 1),)),
        "send_c": dma((2 * (n_col - 1),)),
        "recv_c": dma((2 * (n_col - 1),)),
        "send_d": dma((n_row - 1,)),
        "recv_d": dma((n_row - 1,)),
        "send_e": dma((1,)),
        "recv_e": dma((n_row - 1,)),
        "send_f": dma((2,)),
        "recv_f": dma((2,)),
    }
    names = ["emb_hbm", "kernel_hbm", "cot_hbm", *outputs, *scratch]

    def tile(*refs):
        tile_kernel(n_row, n_col, chunk, types.SimpleNamespace(**dict(zip(names, refs))))

    prediction, grad_kernel, grad_bins = pl.pallas_call(
        tile,
        out_shape=tuple(outputs.values()),
        in_specs=[HBM, HBM, HBM],
        out_specs=(VMEM, VMEM, VMEM),
        scratch_shapes=list(scratch.values()),
        compiler_params=pltpu.CompilerParams(
            collective_id=0, has_side_effects=True, vmem_limit_bytes=32 * 2**20
        ),
        name="tile_gradients",
    )(*[in_hbm(x) for x in (embedding, kernel, cotangent.transpose(1, 2, 0))])

    prediction, grad_kernel, grad_bins = pl.pallas_call(
        functools.partial(finish_kernel, bins),
        out_shape=tuple(outputs.values()),
        in_specs=[VMEM, VMEM, VMEM],
        out_specs=(HBM, HBM, HBM),
        scratch_shapes=[
            pltpu.VMEM((taps, channels), f32),
            pltpu.VMEM((rows, lanes), f32),
            dma((3,)),
        ],
        compiler_params=pltpu.CompilerParams(vmem_limit_bytes=24 * 2**20),
        name="finish",
    )(prediction, grad_kernel, grad_bins)
    return prediction.transpose(2, 0, 1), grad_kernel.reshape(kernel.shape), grad_bins


def solution(mesh):
    in_specs = (P("row", None), P(), P("row", "col", None))
    out_specs = (P("row", "col", None), P(), P("row", None))
    return jax.shard_map(
        functools.partial(on_device, mesh.shape["row"], mesh.shape["col"]),
        mesh=mesh,
        in_specs=in_specs,
        out_specs=out_specs,
        check_vma=False,
    )
```
